128 devices in a mesh: expert: 8 (over x, core), fsdp: 16 (over z, y).
Axes of the slice: x: 4, y: 4, z: 4, core: 2. Of those that a mesh axis runs over, the one named last changes fastest.
Arguments:
- tokens: bfloat16 [2, 4096, 1440], P(None, ('expert', 'fsdp')), may hold values from -6 to 6
- gate_weight: float32 [64, 1440, 1440], P('expert', 'fsdp'), may hold values from -0.15625 to 0.15625
- up_weight: float32 [64, 1440, 1440], P('expert', 'fsdp'), may hold values from -0.15625 to 0.15625
- slot_of: int32 [64], replicated, may hold values from 0 to 127, as said below
- routes: int32 [2, 4096, 4], P(None, 'expert'), may hold values from 0 to 63, all different within a row; in each aligned block of 512 rows (0 to 511, 512 to 1023, ..., all dimensions but the last counted through in order) at most 36 rows name the same one
- route_weight: float32 [2, 4096, 4], P(None, 'expert'), may hold values from 0.05 to 1
Outputs:
- merged: bfloat16 [128, 2880, 1440], P('expert', 'fsdp')
- weighted_hidden: bfloat16 [2, 4096, 4, 1440], P(None, 'expert', None, 'fsdp')
The draws below stay inside these ranges and needn't reach their ends.
Inputs may be any that keep to these rules, and one draw needn't show every extreme that they name: slot_of is one to one. The 8 experts e with the same e // 8 go to 4 owners, exactly 2 to each; one owner receives 2 experts from every such group, so that all its 16 slots are taken. The routes of one row are distinct. In each step, the rows of one index of expert (aligned blocks of 512 rows) name no expert more than 36 times, a bound that some block reaches.
All inputs are finite; a program needn't handle non-finite values.
Results may differ from the reference program's by a relative error of at most 0.0064.
Values may be sent and summed in bfloat16 or wider, within the bound.
A program may use at most 256 MiB of HBM per device.

```python
import math
import jax
import jax.numpy as jnp
import numpy as np
from jax import lax

D = 1440
FF = 1440
EXP_DEV = 8
TOPK = 4
KSEND = 2
STEPS = 2
ROWS_DEV = 32
EXPERTS = 64
SLOTS = 128
ROWS = 4096
MOSTG = 36
N_EXPERT = 8
N_FSDP = 16


def draw_slot_of(key, part):
    key = jax.random.fold_in(key, 11)
    keys_four = jax.random.split(key, 4)
    hot_owner = jax.random.randint(keys_four[0], (), 0, N_EXPERT)
    offset = jax.random.randint(keys_four[1], (), 0, N_EXPERT - 1)
    sources = jnp.arange(N_EXPERT, dtype=jnp.int32)
    local_pos = jnp.arange(EXP_DEV, dtype=jnp.int32)
    choose = local_pos // KSEND
    cycled = (offset + sources[:, None] + choose[None, :] + N_EXPERT - 2) % (N_EXPERT - 1)
    other_owner = (hot_owner + 1 + cycled) % N_EXPERT
    owner_pick = jnp.where(choose[None, :] == 0, hot_owner, other_owner)
    slot_perm = jax.random.permutation(keys_four[2], KSEND * N_EXPERT).astype(jnp.int32)
    inner = slot_perm[sources[:, None] * KSEND + (local_pos % KSEND)[None, :]]
    values = owner_pick * (KSEND * N_EXPERT) + inner
    perms = jax.vmap(lambda one_key: jax.random.permutation(one_key, EXP_DEV))(jax.random.split(keys_four[3], N_EXPERT)).astype(jnp.int32)
    experts_at = sources[:, None] * EXP_DEV + perms
    return jnp.zeros((EXP_DEV * N_EXPERT,), jnp.int32).at[experts_at.reshape(-1)].set(values.reshape(-1).astype(jnp.int32))


def steps_of(own_key, shape, shards, smallest, top_value):
    factor_of = 1.0
    for axis_at, shards_of in shards:
        heights = jax.random.uniform(jax.random.fold_in(jax.random.fold_in(own_key, 6), axis_at), (shards_of,), jnp.float32, smallest / len(shards), top_value / len(shards))
        factor_of = factor_of * jnp.repeat(jnp.exp(heights), shape[axis_at] // shards_of).reshape((-1,) + (1,) * (len(shape) - 1 - axis_at))
    return factor_of


def shared_out(stream_key, own, number, rows, amount, top, most, skew):
    sequence = jax.random.permutation(stream_key, amount)
    heavy_load, common = load_shares(amount, rows * top, most, skew, True), load_shares(amount, rows * top, most, skew, False)
    places = jnp.arange(amount)

    def named(sizes, rotation):
        used = int((sizes > 0).sum())
        fixed = max(1, used // 4)
        moved = fixed + (places - fixed + rotation * (used - fixed)) % max(1, amount - fixed)
        return jnp.zeros((amount,), jnp.int32).at[sequence[jnp.where(places < fixed, places, moved)]].set(jnp.asarray(sizes, jnp.int32))

    sizes = jnp.where(number % 4 == 0, named(heavy_load, number // 4), named(common, number - number // 4 - 1))
    mixed = jax.random.permutation(jax.random.fold_in(own, 3), amount)
    giver, taker = mixed[0:amount // 2 * 2:2], mixed[1:amount // 2 * 2:2]
    room = jnp.minimum(sizes[giver] - 1, most - sizes[taker]) // 2
    room = jnp.where((giver == sequence[0]) | (taker == sequence[0]) | (sizes[taker] == 0), 0, jnp.maximum(room, 0))
    moved = jax.random.randint(jax.random.fold_in(own, 4), (amount // 2,), 0, 1 << 20) % (room + 1)
    sizes = sizes.at[giver].add(-moved).at[taker].add(moved)
    items = jnp.searchsorted(jnp.cumsum(sizes), jnp.arange(rows * top), side="right").astype(jnp.int32)
    listing = items.reshape(top, rows).T
    listing = listing[jax.random.permutation(jax.random.fold_in(own, 1), rows)]
    rotation = jax.random.randint(jax.random.fold_in(own, 2), (rows, 1), 0, top)
    return jnp.take_along_axis(listing, (jnp.arange(top)[None, :] + rotation) % top, axis=1)


def load_shares(amount, total, reach, skew, full):
    weights = [(1 << 20) // math.isqrt(grade ** skew) + 1 for grade in range(1, amount + 1)]
    largest = reach if full else min(reach, max(-(-total // amount), total * weights[0] // sum(weights)))
    least = 1 if total - largest >= amount - 1 else 0
    given, spare = [largest] + [least] * (amount - 1), total - largest - least * (amount - 1)
    while spare > 0:
        free = [i for i in range(1, amount) if given[i] < largest] or [i for i in range(1, amount) if given[i] < reach]
        pool, remaining = sum([weights[i] for i in free]), spare
        for i in free:
            extra = min(reach - given[i], max(1, remaining * weights[i] // pool), spare)
            given[i] = given[i] + extra
            spare = spare - extra
    return np.array(given)


def bell_draw(key, dims, deviation, limit, pieces=(), kind=jnp.bfloat16):
    array = deviation * jax.random.normal(key, dims, jnp.float32)
    if pieces:
        array = array * steps_of(key, dims, pieces, -0.22, 0.18)
    return jnp.clip(array, -limit, limit).astype(kind)


def setup_inputs(seed: int = 0) -> dict:
    key_of = jax.random.split(jax.random.key(seed), 7)
    tokens = bell_draw(key_of[0], (STEPS, ROWS, D), 1.0, 6.0, ((1, 128),))
    gate_weight = bell_draw(key_of[1], (EXPERTS, D, FF), D ** -0.5, 0.15625, ((0, 8), (1, 16)), jnp.float32)
    up_weight = bell_draw(key_of[2], (EXPERTS, D, FF), D ** -0.5, 0.15625, ((0, 8), (1, 16)), jnp.float32)
    slot_of = draw_slot_of(jax.random.fold_in(key_of[6], 71), 0)
    routes_keys = jax.random.split(jax.random.fold_in(key_of[4], 1), STEPS * ROWS // (ROWS_DEV * N_FSDP))
    routes_turns = jax.random.permutation(jax.random.fold_in(key_of[4], 3), STEPS * ROWS // (ROWS_DEV * N_FSDP))
    routes = jax.vmap(lambda own, number: shared_out(jax.random.fold_in(key_of[4], 2), own, number, ROWS_DEV * N_FSDP, EXPERTS, TOPK, MOSTG, 1))(routes_keys, routes_turns).reshape((STEPS, ROWS, TOPK))
    route_weight = jnp.clip(jnp.exp(math.log(1.0) - 2.9957323 * jax.random.uniform(key_of[5], (STEPS, ROWS, TOPK), jnp.float32) ** steps_of(key_of[5], (STEPS, ROWS, TOPK), ((1, 8),), -0.2, 0.2)), 0.05, 1.0)
    return dict(tokens=tokens, gate_weight=gate_weight, up_weight=up_weight, slot_of=slot_of, routes=routes, route_weight=route_weight)


def mix(gate_weight, up_weight):
    paired = jnp.stack([gate_weight.astype(jnp.bfloat16), up_weight.astype(jnp.bfloat16)], axis=-1)
    paired = jnp.transpose(paired, (0, 2, 3, 1))
    return paired.reshape(paired.shape[0], 2 * paired.shape[1], paired.shape[3])


def reference(tokens, gate_weight, up_weight, slot_of, routes, route_weight):
    blocks = mix(gate_weight, up_weight)
    expert_ids = jnp.arange(EXPERTS, dtype=jnp.int32)
    holder = jnp.full((SLOTS,), EXPERTS, jnp.int32).at[slot_of].set(expert_ids)
    padded = jnp.concatenate([blocks, jnp.zeros((1, 2 * FF, D), jnp.bfloat16)], axis=0)
    merged = padded[holder]
    bound_rows = MOSTG * N_EXPERT
    outputs = []
    for step_id in range(STEPS):
        flat_routes = routes[step_id].reshape(-1)
        step_rows = tokens[step_id]

        def one_expert(expert_id):
            picked = jnp.nonzero(flat_routes == expert_id, size=bound_rows, fill_value=0)[0].astype(jnp.int32)
            inputs = step_rows[picked // TOPK]
            weights = lax.dynamic_index_in_dim(blocks, expert_id, 0, keepdims=False)
            projected = jnp.dot(inputs, weights.T, preferred_element_type=jnp.float32)
            hidden = (jax.nn.silu(projected[:, 0::2]) * projected[:, 1::2]).astype(jnp.bfloat16)
            return picked, hidden

        picked, hidden = lax.map(one_expert, expert_ids)
        counts = jnp.sum((flat_routes[None, :] == expert_ids[:, None]).astype(jnp.int32), axis=1)
        usable = jnp.arange(bound_rows, dtype=jnp.int32)[None, :] < counts[:, None]
        targets = jnp.where(usable, picked, ROWS * TOPK).reshape(-1)
        placed = jnp.zeros((ROWS * TOPK + 1, FF), jnp.bfloat16).at[targets].set(hidden.reshape(-1, FF))
        placed = placed[: ROWS * TOPK].reshape(ROWS, TOPK, FF)
        outputs.append((route_weight[step_id][..., None] * placed.astype(jnp.float32)).astype(jnp.bfloat16))
    return merged, jnp.stack(outputs, axis=0)
```

```python
import functools
import jax
import jax.numpy as jnp
from jax import lax
from jax.experimental import pallas as pl
from jax.experimental.pallas import tpu as pltpu
from jax.sharding import PartitionSpec as P

MESH = pl.DeviceIdType.MESH
EXP = 8
PAIRS = 4
GROUPS = 16
OWNERS = 8
SLOTS_DEV = 16
DEPTH = 90
UNITS = 90
WIDTH = 1440
MOST = 36
PLACES = 40
LANES = 384
VMEM_LIMIT = 60 << 20
PEERS = ((2, 0), (1, 0), (3, 0), (2, 1), (1, 1), (3, 1), (0, 1), (0, 0))
FSDP_PEERS = tuple((z, y) for z in range(4) for y in range(4) if (z, y) != (0, 0))


def step_of(source, owner):
    dx = (owner // 2 - source // 2) & 3
    dc = (owner - source) & 1
    near = jnp.where(dx == 2, 0, jnp.where(dx == 1, 1, 2))
    return jnp.where(dx == 0, 7 - dc, 3 * dc + near)


def expert_peer(position, offset):
    dx, dc = offset
    return ((position // 2 + dx) & 3) * 2 + ((position + dc) & 1)


def fsdp_peer(place, offset):
    dz, dy = offset
    return ((place // 4 + dz) & 3) * 4 + ((place + dy) & 3)


def greet(position, place, with_fsdp):
    barrier = pltpu.get_barrier_semaphore()
    count = 0
    for offset in PEERS[:-1]:
        pl.semaphore_signal(
            barrier, inc=1, device_id=(expert_peer(position, offset), place), device_id_type=MESH
        )
        count += 1
    if with_fsdp:
        for offset in FSDP_PEERS:
            pl.semaphore_signal(
                barrier, inc=1, device_id=(position, fsdp_peer(place, offset)), device_id_type=MESH
            )
            count += 1
    pl.semaphore_wait(barrier, count)


def handover_kernel(
    slot_ref, gate_ref, up_ref, routes_ref, weights_ref, arrived_ref, all_routes_ref,
    raw, ranked, send, recv, tall, blocks, xsend,
    load_sem, send_sem, recv_sem, xsend_sem, xrecv_sem, own_sem, rsend_sem, rrecv_sem, rown_sem,
):
    position = lax.axis_index("expert")
    place = lax.axis_index("fsdp")
    loads = [
        pltpu.make_async_copy(ref, raw.at[w], load_sem.at[w])
        for w, ref in enumerate((gate_ref, up_ref))
    ]
    for load in loads:
        load.start()
    greet(position, place, True)

    def routes_copy(k):
        return pltpu.make_async_remote_copy(
            src_ref=routes_ref,
            dst_ref=all_routes_ref.at[position],
            send_sem=rsend_sem.at[k],
            recv_sem=rrecv_sem.at[position],
            device_id=(expert_peer(position, PEERS[k]), place),
            device_id_type=MESH,
        )

    def routes_arrival(k):
        source = expert_peer(position, PEERS[k])
        return pltpu.make_async_remote_copy(
            src_ref=routes_ref,
            dst_ref=all_routes_ref.at[source],
            send_sem=rsend_sem.at[k],
            recv_sem=rrecv_sem.at[source],
            device_id=(source, place),
            device_id_type=MESH,
        )

    for k in range(7):
        routes_copy(k).start()
    own_routes = pltpu.make_async_copy(routes_ref, all_routes_ref.at[position], rown_sem)
    own_routes.start()

    keys = []
    for j in range(EXP):
        owner = slot_ref[position * EXP + j] // SLOTS_DEV
        keys.append(step_of(position, owner) * EXP + j)
    order = [0] * EXP
    step_at = [0] * EXP
    for j in range(EXP):
        rank = 0
        for other in range(EXP):
            if other != j:
                rank = rank + (keys[other] < keys[j]).astype(jnp.int32)
        for i in range(EXP):
            here = (rank == i).astype(jnp.int32)
            order[i] = order[i] + here * j
            step_at[i] = step_at[i] + here * (keys[j] // EXP)
    pair_of = []
    for k in range(OWNERS):
        found = 0
        for p in range(PAIRS):
            found = jnp.where(step_at[2 * p] == k, p, found)
        pair_of.append(found)

    def piece_copy(p, offset):
        target = fsdp_peer(place, offset)
        return pltpu.make_async_remote_copy(
            src_ref=send.at[p, target],
            dst_ref=recv.at[p, place],
            send_sem=send_sem.at[p, target],
            recv_sem=recv_sem.at[p, place],
            device_id=(position, target),
            device_id_type=MESH,
        )

    def piece_arrival(p, offset):
        source = fsdp_peer(place, offset)
        return pltpu.make_async_remote_copy(
            src_ref=send.at[p, source],
            dst_ref=recv.at[p, source],
            send_sem=send_sem.at[p, source],
            recv_sem=recv_sem.at[p, source],
            device_id=(position, source),
            device_id_type=MESH,
        )

    to = lax.broadcasted_iota(jnp.int32, (128, 128), 0)
    at = lax.broadcasted_iota(jnp.int32, (128, 128), 1)
    named = jnp.zeros((128, 128), jnp.int32)
    for i in range(EXP):
        named = jnp.where((to >> 4) == i, order[i], named)
    rank_rows = ((to & 15) == (at >> 3)) & (named == (at & 7))
    rank_rows = rank_rows.astype(jnp.float32).astype(jnp.bfloat16)
    for w in range(2):
        loads[w].wait()
        for c in range(6):
            depth = min(16, DEPTH - 16 * c)
            some = raw[w, 16 * c:16 * c + depth].reshape(depth * EXP, WIDTH).astype(jnp.bfloat16)
            put = jnp.dot(rank_rows[:, :depth * EXP], some, preferred_element_type=jnp.float32)
            ranked[w, :, 16 * c:16 * c + 16, :] = put.astype(jnp.bfloat16).reshape(EXP, 16, WIDTH)

    pad = jnp.zeros((96, LANES - 4 * UNITS), jnp.bfloat16)
    for p in range(PAIRS):
        for f in range(GROUPS):
            units = slice(f * UNITS, (f + 1) * UNITS)
            send[p, f] = jnp.concatenate(
                [
                    ranked[0, 2 * p, :, units],
                    ranked[1, 2 * p, :, units],
                    ranked[0, 2 * p + 1, :, units],
                    ranked[1, 2 * p + 1, :, units],
                    pad,
                ],
                axis=1,
            )
        for offset in FSDP_PEERS:
            piece_copy(p, offset).start()
        recv[p, place] = send[p, place]

    row = lax.broadcasted_iota(jnp.int32, (384, LANES), 0)
    lane = lax.broadcasted_iota(jnp.int32, (384, LANES), 1)
    second = (row >= 192).astype(jnp.int32)
    inner = row - 192 * second
    wanted = jnp.where(inner < 180, 180 * second + 90 * (inner & 1) + (inner >> 1), -1)
    mix = (lane == wanted).astype(jnp.float32).astype(jnp.bfloat16)

    def xcopy(k):
        return pltpu.make_async_remote_copy(
            src_ref=xsend.at[k],
            dst_ref=arrived_ref.at[k],
            send_sem=xsend_sem.at[k],
            recv_sem=xrecv_sem.at[k],
            device_id=(expert_peer(position, PEERS[k]), place),
            device_id_type=MESH,
        )

    own_copy = pltpu.make_async_copy(xsend.at[7], arrived_ref.at[7], own_sem)
    for p in range(PAIRS):
        for offset in FSDP_PEERS:
            piece_arrival(p, offset).wait_recv()
        for f in range(GROUPS):
            tall[f * DEPTH:(f + 1) * DEPTH, :] = recv[p, f, 0:DEPTH, :].astype(jnp.float32)
        whole = tall[...].astype(jnp.bfloat16)
        weights_ref[p] = whole
        turned = lax.dot_general(
            mix, whole, (((1,), (1,)), ((), ())), preferred_element_type=jnp.float32
        )
        blocks[p, 0] = turned[0:180].astype(jnp.bfloat16)
        blocks[p, 1] = turned[192:372].astype(jnp.bfloat16)
        for k in (p,) if p < PAIRS - 1 else range(PAIRS - 1, OWNERS):
            xsend[k] = blocks[pair_of[k]]
            if k < 7:
                xcopy(k).start()
            else:
                own_copy.start()
    for k in range(7):
        xcopy(k).wait()
        routes_arrival(k).wait_recv()
        routes_copy(k).wait_send()
    own_copy.wait()
    own_routes.wait()
    for p in range(PAIRS):
        for offset in FSDP_PEERS:
            piece_copy(p, offset).wait_send()


def compute_kernel(
    ids_ref, routes_ref, weights_ref, tokens_ref, hidden_ref,
    chunk, spots, rows, hsend, chunk_sem, send_sem, recv_sem, own_sem,
):
    position = lax.axis_index("expert")
    place = lax.axis_index("fsdp")

    def fetch(s):
        return pltpu.make_async_copy(
            tokens_ref.at[pl.ds(s * GROUPS, GROUPS)], chunk.at[s % 2], chunk_sem.at[s % 2]
        )

    fetch(0).start()
    greet(position, place, False)
    ids = ids_ref[:, 0:1]
    masks = []
    for s in range(OWNERS):
        for t in range(2):
            named = routes_ref[s, t]
            mask = jnp.zeros((EXP, 512), jnp.float32)
            for k in range(4):
                mask = mask + (named[k:k + 1, :] == ids).astype(jnp.float32)
            masks.append(mask)
    mask = jnp.concatenate(masks, axis=0)
    before = (
        lax.broadcasted_iota(jnp.int32, (512, 512), 0) < lax.broadcasted_iota(jnp.int32, (512, 512), 1)
    ).astype(jnp.float32).astype(jnp.bfloat16)
    earlier = jnp.dot(mask.astype(jnp.bfloat16), before, preferred_element_type=jnp.float32)
    spots[...] = jnp.where(mask > 0.5, earlier, -1.0).reshape(16, EXP, 512)

    nth = lax.broadcasted_iota(jnp.int32, (EXP, PLACES, 512), 1).astype(jnp.float32)
    for s in range(OWNERS):
        fetch(s).wait()
        if s + 1 < OWNERS:
            fetch(s + 1).start()
        picked = []
        for t in range(2):
            spot = spots[2 * s + t]
            choose = (spot[:, None, :] == nth).astype(jnp.float32)
            choose = choose.reshape(EXP * PLACES, 512).astype(jnp.bfloat16)
            step_tokens = chunk[s % 2, :, t].reshape(512, WIDTH)
            picked.append(jnp.dot(choose, step_tokens, preferred_element_type=jnp.float32))
        for j in range(EXP):
            both = jnp.concatenate(
                [one[j * PLACES:(j + 1) * PLACES] for one in picked], axis=0
            )
            rows[j, s * 2 * PLACES:(s + 1) * 2 * PLACES, :] = both.astype(jnp.bfloat16)

    for j in range(EXP):
        projected = jnp.dot(rows[j], weights_ref[j // 2], preferred_element_type=jnp.float32)
        start = 180 * (j % 2)
        gate = projected[:, start:start + UNITS]
        up = projected[:, start + UNITS:start + 2 * UNITS]
        hidden = (gate / (1.0 + jnp.exp(-gate)) * up).astype(jnp.bfloat16)
        hidden = hidden.reshape(OWNERS, 2 * PLACES, UNITS)
        hsend[:, j * 2 * PLACES:(j + 1) * 2 * PLACES, 0:UNITS] = hidden

    def give(k):
        target = expert_peer(position, PEERS[k])
        return pltpu.make_async_remote_copy(
            src_ref=hsend.at[target],
            dst_ref=hidden_ref.at[position],
            send_sem=send_sem.at[target],
            recv_sem=recv_sem.at[position],
            device_id=(target, place),
            device_id_type=MESH,
        )

    def get(k):
        source = expert_peer(position, PEERS[k])
        return pltpu.make_async_remote_copy(
            src_ref=hsend.at[source],
            dst_ref=hidden_ref.at[source],
            send_sem=send_sem.at[source],
            recv_sem=recv_sem.at[source],
            device_id=(source, place),
            device_id_type=MESH,
        )

    for k in range(7):
        give(k).start()
    own = pltpu.make_async_copy(hsend.at[position], hidden_ref.at[position], own_sem)
    own.start()
    own.wait()
    for k in range(7):
        get(k).wait_recv()
        give(k).wait_send()


def merge_kernel(from_ref, arrived_ref, merged_ref, select):
    part = pl.program_id(0)

    @pl.when(part == 0)
    def _():
        to = lax.broadcasted_iota(jnp.int32, (256, 256), 0)
        at = lax.broadcasted_iota(jnp.int32, (256, 256), 1)
        named = jnp.zeros((256, 256), jnp.int32)
        for q in range(SLOTS_DEV):
            named = jnp.where((to & 15) == q, from_ref[q], named)
        hit = ((to >> 4) == (at & 15)) & (named == (at >> 4))
        select[...] = hit.astype(jnp.float32).astype(jnp.bfloat16)

    there = lax.broadcasted_iota(jnp.int32, (16, 16, WIDTH), 1) + part * 16 < 180
    some = jnp.where(there, arrived_ref[...], jnp.zeros((), jnp.bfloat16))
    put = jnp.dot(select[...], some.reshape(256, WIDTH), preferred_element_type=jnp.float32)
    merged_ref[...] = put.astype(jnp.bfloat16).reshape(16, SLOTS_DEV, WIDTH)


def combine_kernel(routes_ref, route_weight_ref, base_ref, hidden_ref, out_ref, spread):
    held = hidden_ref[...].astype(jnp.float32).reshape(EXP * OWNERS, 2 * PLACES, 128)
    before = (
        lax.broadcasted_iota(jnp.int32, (512, 512), 0) < lax.broadcasted_iota(jnp.int32, (512, 512), 1)
    ).astype(jnp.float32).astype(jnp.bfloat16)
    expert = lax.broadcasted_iota(jnp.int32, (64, 512), 0)
    table = 64 * PLACES
    index = lax.broadcasted_iota(jnp.int32, (table, 512), 0)
    for t in range(2):
        step = held[:, t * PLACES:(t + 1) * PLACES].reshape(table, 128).astype(jnp.bfloat16)
        turned = jnp.transpose(step)
        named = [(routes_ref[t, k:k + 1, :] == expert).astype(jnp.float32) for k in range(4)]
        mask = named[0] + named[1] + named[2] + named[3]
        earlier = jnp.dot(mask.astype(jnp.bfloat16), before, preferred_element_type=jnp.float32)
        at = earlier + base_ref[:, 0:1]
        for k in range(4):
            code = jnp.sum(named[k] * at, axis=0, keepdims=True).astype(jnp.int32)
            choose = (index == code).astype(jnp.float32).astype(jnp.bfloat16)
            hidden = jnp.dot(turned, choose, preferred_element_type=jnp.float32)
            weighted = route_weight_ref[t, k:k + 1, :] * hidden[0:UNITS]
            for part in range(4):
                spread[part, pl.ds(k, UNITS, stride=4), :] = weighted[:, part * 128:(part + 1) * 128]
        for part in range(4):
            out_ref[t, :, part * 128:(part + 1) * 128] = spread[part].astype(jnp.bfloat16)


def on_device(tokens, gate_weight, up_weight, slot_of, routes, route_weight):
    position = lax.axis_index("expert")
    ids = jnp.arange(64, dtype=jnp.int32)
    source = ids // EXP
    owner = slot_of // SLOTS_DEV
    step = step_of(source, owner)
    key = step * EXP + ids % EXP
    ahead = (source[None, :] == source[:, None]) & (key[None, :] < key[:, None])
    rank = jnp.sum(ahead.astype(jnp.int32), axis=1)
    within = jnp.sum((ahead & (step[None, :] == step[:, None])).astype(jnp.int32), axis=1)
    at = step * 2 + within
    mine = slot_of[None, :] == (position * SLOTS_DEV + jnp.arange(SLOTS_DEV, dtype=jnp.int32))[:, None]
    from_ = jnp.max(jnp.where(mine, at[None, :], -1), axis=1)
    local = (source[None, :] == position) & (rank[None, :] == jnp.arange(EXP, dtype=jnp.int32)[:, None])
    local_ids = jnp.sum(jnp.where(local, ids[None, :], 0), axis=1)
    local_ids = jnp.broadcast_to(local_ids[:, None], (EXP, 128))
    base = ((source * EXP + rank) * PLACES).astype(jnp.float32)
    base = jnp.broadcast_to(base[:, None], (64, 128))

    all_tokens = lax.all_gather(tokens, ("expert", "fsdp"), axis=0)
    routes = jnp.swapaxes(routes, 1, 2)
    route_weight = jnp.swapaxes(route_weight, 1, 2)

    vmem = pl.BlockSpec(memory_space=pltpu.VMEM)
    smem = pl.BlockSpec(memory_space=pltpu.SMEM)
    anyspace = pl.BlockSpec(memory_space=pl.ANY)
    bf16 = jnp.bfloat16
    weights, arrived, all_routes = pl.pallas_call(
        handover_kernel,
        out_shape=(
            jax.ShapeDtypeStruct((PAIRS, WIDTH, LANES), bf16),
            jax.ShapeDtypeStruct((OWNERS, 2, 180, WIDTH), bf16),
            jax.ShapeDtypeStruct((OWNERS, 2, 4, 512), jnp.int32),
        ),
        in_specs=[smem, anyspace, anyspace, anyspace],
        out_specs=(vmem, anyspace, anyspace),
        scratch_shapes=[
            pltpu.VMEM((2, DEPTH, EXP, WIDTH), jnp.float32),
            pltpu.VMEM((2, EXP, 96, WIDTH), bf16),
            pltpu.VMEM((PAIRS, GROUPS, 96, LANES), bf16),
            pltpu.VMEM((PAIRS, GROUPS, 96, LANES), bf16),
            pltpu.VMEM((WIDTH, LANES), jnp.float32),
            pltpu.VMEM((PAIRS, 2, 180, WIDTH), bf16),
            pltpu.VMEM((OWNERS, 2, 180, WIDTH), bf16),
            pltpu.SemaphoreType.DMA((2,)),
            pltpu.SemaphoreType.DMA((PAIRS, GROUPS)),
            pltpu.SemaphoreType.DMA((PAIRS, GROUPS)),
            pltpu.SemaphoreType.DMA((7,)),
            pltpu.SemaphoreType.DMA((7,)),
            pltpu.SemaphoreType.DMA,
            pltpu.SemaphoreType.DMA((7,)),
            pltpu.SemaphoreType.DMA((OWNERS,)),
            pltpu.SemaphoreType.DMA,
        ],
        compiler_params=pltpu.CompilerParams(
            collective_id=1, has_side_effects=True, vmem_limit_bytes=VMEM_LIMIT
        ),
        cost_estimate=pl.CostEstimate(flops=2 * 10**9, bytes_accessed=400 * 10**6, transcendentals=0),
        name="handover",
    )(slot_of, jnp.swapaxes(gate_weight, 0, 1), jnp.swapaxes(up_weight, 0, 1), routes)

    hidden = pl.pallas_call(
        compute_kernel,
        out_shape=jax.ShapeDtypeStruct((OWNERS, EXP * 2 * PLACES, 128), bf16),
        in_specs=[vmem, vmem, vmem, anyspace],
        out_specs=anyspace,
        scratch_shapes=[
            pltpu.VMEM((2, GROUPS, 2, 32, WIDTH), bf16),
            pltpu.VMEM((16, EXP, 512), jnp.float32),
            pltpu.VMEM((EXP, OWNERS * 2 * PLACES, WIDTH), bf16),
            pltpu.VMEM((OWNERS, EXP * 2 * PLACES, 128), bf16),
            pltpu.SemaphoreType.DMA((2,)),
            pltpu.SemaphoreType.DMA((OWNERS,)),
            pltpu.SemaphoreType.DMA((OWNERS,)),
            pltpu.SemaphoreType.DMA,
        ],
        compiler_params=pltpu.CompilerParams(
            collective_id=2, has_side_effects=True, vmem_limit_bytes=VMEM_LIMIT
        ),
        cost_estimate=pl.CostEstimate(flops=12 * 10**9, bytes_accessed=30 * 10**6, transcendentals=10**6),
        name="project",
    )(local_ids, all_routes, weights, all_tokens)

    merged = pl.pallas_call(
        merge_kernel,
        out_shape=jax.ShapeDtypeStruct((180, SLOTS_DEV, WIDTH), bf16),
        grid_spec=pltpu.PrefetchScalarGridSpec(
            num_scalar_prefetch=1,
            grid=(12,),
            in_specs=[pl.BlockSpec((SLOTS_DEV, 16, WIDTH), lambda i, from_ref: (0, i, 0))],
            out_specs=pl.BlockSpec((16, SLOTS_DEV, WIDTH), lambda i, from_ref: (i, 0, 0)),
            scratch_shapes=[pltpu.VMEM((256, 256), bf16)],
        ),
        compiler_params=pltpu.CompilerParams(vmem_limit_bytes=VMEM_LIMIT),
        name="merge",
    )(from_, arrived.reshape(SLOTS_DEV, 180, WIDTH))
    weighted = pl.pallas_call(
        combine_kernel,
        out_shape=jax.ShapeDtypeStruct((2, 4 * UNITS, 512), bf16),
        in_specs=[vmem, vmem, vmem, vmem],
        out_specs=vmem,
        scratch_shapes=[pltpu.VMEM((4, 4 * UNITS, 128), jnp.float32)],
        compiler_params=pltpu.CompilerParams(vmem_limit_bytes=VMEM_LIMIT),
        name="combine",
    )(routes, route_weight, base, hidden)
    weighted = weighted.reshape(2, UNITS, 4, 512)
    return jnp.swapaxes(merged, 0, 1), jnp.transpose(weighted, (0, 3, 2, 1))


def solution(mesh):
    in_specs = (
        P(None, ("expert", "fsdp"), None),
        P("expert", "fsdp", None),
        P("expert", "fsdp", None),
        P(),
        P(None, "expert", None),
        P(None, "expert", None),
    )
    out_specs = (P("expert", "fsdp", None), P(None, "expert", None, "fsdp"))
    return jax.shard_map(
        on_device, mesh=mesh, in_specs=in_specs, out_specs=out_specs, check_vma=False
    )
```

```python
import functools
import jax
import jax.numpy as jnp
from jax import lax
from jax.experimental import pallas as pl
from jax.experimental.pallas import tpu as pltpu
from jax.sharding import PartitionSpec as P

MESH = pl.DeviceIdType.MESH
EXP = 8
PAIRS = 4
GROUPS = 16
OWNERS = 8
SLOTS_DEV = 16
DEPTH = 90
UNITS = 90
WIDTH = 1440
MOST = 36
PLACES = 40
LANES = 384
MAIN = 1408
TAIL = WIDTH - MAIN
HALF = 4
VMEM_LIMIT = 60 << 20
PEERS = ((2, 0), (1, 0), (3, 0), (2, 1), (1, 1), (3, 1), (0, 1), (0, 0))
FSDP_PEERS = (
    (0, 1), (3, 0), (0, 3), (1, 0), (1, 1), (3, 3), (1, 3), (3, 1),
    (2, 0), (0, 2), (2, 1), (1, 2), (2, 3), (3, 2), (2, 2),
)
WAVES = 2
SCHEDULE = (
    "P0", "P1", "P2", "P3", "L0", "S0", "S1", "A0", "A1", "A2", "A3",
    "N0", "N1", "F0", "F1", "l0", "l1", "f0", "R0", "C0", "G0", "G1", "G2", "G3", "f1", "M0",
    "C1", "G4", "G5", "G6", "G7", "M1",
)


def step_of(source, owner):
    dx = (owner // 2 - source // 2) & 3
    dc = (owner - source) & 1
    near = jnp.where(dx == 2, 0, jnp.where(dx == 1, 1, 2))
    return jnp.where(dx == 0, 7 - dc, 3 * dc + near)


def expert_peer(position, offset):
    dx, dc = offset
    return ((position // 2 + dx) & 3) * 2 + ((position + dc) & 1)


def fsdp_peer(place, offset):
    dz, dy = offset
    return ((place // 4 + dz) & 3) * 4 + ((place + dy) & 3)


def greet(position, place, with_fsdp):
    barrier = pltpu.get_barrier_semaphore()
    count = 0
    for offset in PEERS[:-1]:
        pl.semaphore_signal(
            barrier, inc=1, device_id=(expert_peer(position, offset), place), device_id_type=MESH
        )
        count += 1
    if with_fsdp:
        for offset in FSDP_PEERS:
            pl.semaphore_signal(
                barrier, inc=1, device_id=(position, fsdp_peer(place, offset)), device_id_type=MESH
            )
            count += 1
    pl.semaphore_wait(barrier, count)


class TokenGather:
    def __init__(self, tokens, everything, line_send, line_recv, own_sem, send, recv, pair_send, pair_recv):
        self.position = lax.axis_index("expert")
        self.place = lax.axis_index("fsdp")
        self.core = self.position & 1
        self.x = self.position // 2
        self.tokens, self.everything = tokens, everything
        self.line_send, self.line_recv, self.own_sem = line_send, line_recv, own_sem
        self.send, self.recv, self.pair_send, self.pair_recv = send, recv, pair_send, pair_recv
        self.count = 0
        self.sent = []

    def line_copy(self, dx, source_dx):
        x = (self.x + source_dx) & 3
        return pltpu.make_async_remote_copy(
            src_ref=self.tokens,
            dst_ref=self.everything.at[self.core, self.place, x],
            send_sem=self.line_send.at[dx - 1],
            recv_sem=self.line_recv.at[x],
            device_id=(((self.x + dx) & 3) * 2 + self.core, self.place),
            device_id_type=MESH,
        )

    def own_copy(self):
        return pltpu.make_async_copy(
            self.tokens, self.everything.at[self.core, self.place, self.x], self.own_sem
        )

    def begin(self):
        for dx in (2, 1, 3):
            self.line_copy(dx, 0).start()
        self.own_copy().start()

    def line_done(self):
        self.own_copy().wait()
        for dx in (1, 2, 3):
            self.line_copy(dx, dx).wait_recv()

    def at(self, kind, first, second):
        return fsdp_peer(self.place, (second, first) if kind == 0 else (first, second))

    def unit(self, wave, kind, f, half, core):
        ref = self.everything.at[core, f, 2 * wave + kind]
        return ref if half is None else ref.at[half]

    def copy(self, wave, kind, f, half, target, index):
        ref = self.unit(wave, kind, f, half, self.core)
        return pltpu.make_async_remote_copy(
            src_ref=ref,
            dst_ref=ref,
            send_sem=self.send.at[index],
            recv_sem=self.recv.at[wave, kind, f, 0 if half is None else half],
            device_id=(self.position, target),
            device_id_type=MESH,
        )

    def give(self, wave, kind, f, half, target):
        copy = self.copy(wave, kind, f, half, target, self.count)
        copy.start()
        self.sent.append(copy)
        self.count += 1

    def arrival(self, wave, kind, f, half):
        self.copy(wave, kind, f, half, self.place, 0).wait_recv()

    def pair_copy(self, wave, kind, f, core):
        ref = self.unit(wave, kind, f, None, core)
        return pltpu.make_async_remote_copy(
            src_ref=ref,
            dst_ref=ref,
            send_sem=self.pair_send.at[wave, kind, f],
            recv_sem=self.pair_recv.at[wave, kind, f],
            device_id=(self.position ^ 1, self.place),
            device_id_type=MESH,
        )

    def share(self, wave, kind, f):
        self.pair_copy(wave, kind, f, self.core).start()

    def across(self, wave, kind, first):
        f = self.at(kind, first, 0)
        for second in (1, 3):
            self.give(wave, kind, f, None, self.at(kind, 0, second))
        self.share(wave, kind, f)

    def start(self, wave):
        for kind in range(2):
            for first in (1, 3):
                self.give(wave, kind, self.place, None, self.at(kind, first, 0))
        for kind in range(2):
            self.across(wave, kind, 0)

    def near(self, wave):
        for kind in range(2):
            for first, half in ((3, 0), (1, 1)):
                f = self.at(kind, first, 0)
                self.arrival(wave, kind, f, None)
                self.give(wave, kind, f, half, self.at(kind, (first + 2) & 3, 0))
        for kind in range(2):
            for first in (3, 1):
                self.across(wave, kind, first)

    def far(self, wave):
        for kind in range(2):
            f = self.at(kind, 2, 0)
            self.arrival(wave, kind, f, 0)
            self.arrival(wave, kind, f, 1)
            self.across(wave, kind, 2)

    def near_lines(self, wave, firsts):
        for first in firsts:
            for kind in range(2):
                for second, half in ((3, 0), (1, 1)):
                    f = self.at(kind, first, second)
                    self.arrival(wave, kind, f, None)
                    self.give(wave, kind, f, half, self.at(kind, 0, (second + 2) & 3))
                    self.share(wave, kind, f)

    def far_lines(self, wave):
        for first in (0, 3, 1, 2):
            for kind in range(2):
                f = self.at(kind, first, 2)
                self.arrival(wave, kind, f, 0)
                self.arrival(wave, kind, f, 1)
                self.share(wave, kind, f)

    def other_core(self, wave):
        for kind in range(2):
            for f in range(GROUPS):
                self.pair_copy(wave, kind, f, 1 - self.core).wait_recv()

    def end(self):
        for dx in (1, 2, 3):
            self.line_copy(dx, 0).wait_send()
        for copy in self.sent:
            copy.wait_send()
        for wave in range(WAVES):
            for kind in range(2):
                for f in range(GROUPS):
                    self.pair_copy(wave, kind, f, self.core).wait_send()


def serve_kernel(
    slot_ref, gate_ref, up_ref, routes_ref, tokens_ref,
    main_ref, tail_ref, hidden_ref, all_tokens_ref,
    raw, ranked, send, recv, tall, weights, blocks, ends, xsend, xends, all_routes, spots, chunk, rows, hsend,
    load_sem, send_sem, recv_sem, xsend_sem, xrecv_sem, own_sem, rsend_sem, rrecv_sem, rown_sem,
    chunk_sem, hsend_sem, hrecv_sem, hown_sem, *gather_sems,
):
    position = lax.axis_index("expert")
    place = lax.axis_index("fsdp")

    def load(i):
        ref = (gate_ref, up_ref)[i // 6]
        start = 16 * (i % 6)
        depth = min(16, DEPTH - start)
        return pltpu.make_async_copy(
            ref.at[pl.ds(start, depth)], raw.at[i % 4, pl.ds(0, depth)], load_sem.at[i % 4]
        )

    for i in range(4):
        load(i).start()
    greet(position, place, True)
    gather = TokenGather(tokens_ref, all_tokens_ref, *gather_sems)
    gather.begin()

    def routes_copy(k):
        return pltpu.make_async_remote_copy(
            src_ref=routes_ref,
            dst_ref=all_routes.at[position],
            send_sem=rsend_sem.at[k],
            recv_sem=rrecv_sem.at[position],
            device_id=(expert_peer(position, PEERS[k]), place),
            device_id_type=MESH,
        )

    def routes_arrival(k):
        source = expert_peer(position, PEERS[k])
        return pltpu.make_async_remote_copy(
            src_ref=routes_ref,
            dst_ref=all_routes.at[source],
            send_sem=rsend_sem.at[k],
            recv_sem=rrecv_sem.at[source],
            device_id=(source, place),
            device_id_type=MESH,
        )

    for k in range(7):
        routes_copy(k).start()
    own_routes = pltpu.make_async_copy(routes_ref, all_routes.at[position], rown_sem)
    own_routes.start()

    keys = []
    for j in range(EXP):
        owner = slot_ref[position * EXP + j] // SLOTS_DEV
        keys.append(step_of(position, owner) * EXP + j)
    order = [0] * EXP
    step_at = [0] * EXP
    for j in range(EXP):
        rank = 0
        for other in range(EXP):
            if other != j:
                rank = rank + (keys[other] < keys[j]).astype(jnp.int32)
        for i in range(EXP):
            here = (rank == i).astype(jnp.int32)
            order[i] = order[i] + here * j
            step_at[i] = step_at[i] + here * (keys[j] // EXP)
    pair_of = []
    for k in range(OWNERS):
        found = 0
        for p in range(PAIRS):
            found = jnp.where(step_at[2 * p] == k, p, found)
        pair_of.append(found)

    def piece_copy(p, offset):
        target = fsdp_peer(place, offset)
        return pltpu.make_async_remote_copy(
            src_ref=send.at[p, target],
            dst_ref=recv.at[p, place],
            send_sem=send_sem.at[p, target],
            recv_sem=recv_sem.at[p, place],
            device_id=(position, target),
            device_id_type=MESH,
        )

    def piece_arrival(p, offset):
        source = fsdp_peer(place, offset)
        return pltpu.make_async_remote_copy(
            src_ref=send.at[p, source],
            dst_ref=recv.at[p, source],
            send_sem=send_sem.at[p, source],
            recv_sem=recv_sem.at[p, source],
            device_id=(position, source),
            device_id_type=MESH,
        )

    to = lax.broadcasted_iota(jnp.int32, (128, 128), 0)
    at = lax.broadcasted_iota(jnp.int32, (128, 128), 1)
    named = jnp.zeros((128, 128), jnp.int32)
    for i in range(EXP):
        named = jnp.where((to >> 4) == i, order[i], named)
    rank_rows = ((to & 15) == (at >> 3)) & (named == (at & 7))
    rank_rows = rank_rows.astype(jnp.float32).astype(jnp.bfloat16)
    for i in range(12):
        load(i).wait()
        c = i % 6
        depth = min(16, DEPTH - 16 * c)
        some = raw[i % 4, 0:depth].reshape(depth * EXP, WIDTH).astype(jnp.bfloat16)
        put = jnp.dot(rank_rows[:, :depth * EXP], some, preferred_element_type=jnp.float32)
        ranked[i // 6, :, 16 * c:16 * c + 16, :] = put.astype(jnp.bfloat16).reshape(EXP, 16, WIDTH)
        if i + 4 < 12:
            load(i + 4).start()

    pad = jnp.zeros((96, LANES - 4 * UNITS), jnp.bfloat16)

    def prepare(p):
        for f in range(GROUPS):
            units = slice(f * UNITS, (f + 1) * UNITS)
            send[p, f] = jnp.concatenate(
                [
                    ranked[0, 2 * p, :, units],
                    ranked[1, 2 * p, :, units],
                    ranked[0, 2 * p + 1, :, units],
                    ranked[1, 2 * p + 1, :, units],
                    pad,
                ],
                axis=1,
            )
        for offset in FSDP_PEERS:
            piece_copy(p, offset).start()
        recv[p, place] = send[p, place]

    row = lax.broadcasted_iota(jnp.int32, (360, LANES), 0)
    lane = lax.broadcasted_iota(jnp.int32, (360, LANES), 1)
    inner = 4 * (row >> 3) + (row & 3)
    mix = lane == 180 * ((row >> 2) & 1) + 90 * (inner & 1) + (inner >> 1)
    mix = mix.astype(jnp.float32).astype(jnp.bfloat16)

    def xcopies(k):
        peer = (expert_peer(position, PEERS[k]), place)
        return [
            pltpu.make_async_remote_copy(
                src_ref=source.at[k],
                dst_ref=target.at[k],
                send_sem=xsend_sem.at[part, k],
                recv_sem=xrecv_sem.at[part, k],
                device_id=peer,
                device_id_type=MESH,
            )
            for part, (source, target) in enumerate(((xsend, main_ref), (xends, tail_ref)))
        ]

    own_copies = [
        pltpu.make_async_copy(xsend.at[7], main_ref.at[7], own_sem.at[0]),
        pltpu.make_async_copy(xends.at[7], tail_ref.at[7], own_sem.at[1]),
    ]

    def assemble(p):
        for offset in FSDP_PEERS:
            piece_arrival(p, offset).wait_recv()
        for f in range(GROUPS):
            tall[f * DEPTH:(f + 1) * DEPTH, :] = recv[p, f, 0:DEPTH, :].astype(jnp.float32)
        whole = tall[...].astype(jnp.bfloat16)
        weights[p] = whole
        turned = lax.dot_general(
            mix, whole, (((1,), (1,)), ((), ())), preferred_element_type=jnp.float32
        )
        blocks[p] = turned[:, 0:MAIN].astype(jnp.bfloat16)
        last = turned[:, MAIN:WIDTH]
        last = jnp.concatenate(
            [
                last[0:128],
                last[128:256],
                jnp.concatenate([last[256:360], jnp.zeros((24, TAIL), jnp.float32)], axis=0),
                jnp.zeros((128, TAIL), jnp.float32),
            ],
            axis=1,
        )
        ends[p] = last.astype(jnp.bfloat16)
        for k in (p,) if p < PAIRS - 1 else range(PAIRS - 1, OWNERS):
            xsend[k] = blocks[pair_of[k]]
            xends[k] = ends[pair_of[k]]
            for copy in xcopies(k) if k < 7 else own_copies:
                copy.start()

    def find_rows(_):
        own_routes.wait()
        for k in range(7):
            routes_arrival(k).wait_recv()
        nth = lax.broadcasted_iota(jnp.int32, (EXP, 512), 0)
        ids = jnp.zeros((EXP, 512), jnp.int32)
        for i in range(EXP):
            ids = jnp.where(nth == i, position * EXP + order[i], ids)
        masks = []
        for s in range(OWNERS):
            for t in range(2):
                named = all_routes[s, t]
                mask = jnp.zeros((EXP, 512), jnp.float32)
                for k in range(4):
                    mask = mask + (named[k:k + 1, :] == ids).astype(jnp.float32)
                masks.append(mask)
        mask = jnp.concatenate(masks, axis=0)
        before = (
            lax.broadcasted_iota(jnp.int32, (512, 512), 0)
            < lax.broadcasted_iota(jnp.int32, (512, 512), 1)
        ).astype(jnp.float32).astype(jnp.bfloat16)
        earlier = jnp.dot(mask.astype(jnp.bfloat16), before, preferred_element_type=jnp.float32)
        spots[...] = jnp.where(mask > 0.5, earlier, -1.0).reshape(16, EXP, 512)

    def fetch(s):
        return pltpu.make_async_copy(
            all_tokens_ref.at[s % 2, :, s // 2], chunk.at[s % 2], chunk_sem.at[s % 2]
        )

    def arrived(wave):
        gather.other_core(wave)
        fetch(HALF * wave).start()
        fetch(HALF * wave + 1).start()

    def pick(s):
        nth = lax.broadcasted_iota(jnp.int32, (EXP, PLACES, 512), 1).astype(jnp.float32)
        fetch(s).wait()
        picked = []
        for t in range(2):
            spot = spots[2 * s + t]
            choose = (spot[:, None, :] == nth).astype(jnp.float32)
            choose = choose.reshape(EXP * PLACES, 512).astype(jnp.bfloat16)
            step_tokens = chunk[s % 2, :, t].reshape(512, WIDTH)
            picked.append(jnp.dot(choose, step_tokens, preferred_element_type=jnp.float32))
        start = (s % HALF) * 2 * PLACES
        for j in range(EXP):
            both = jnp.concatenate([one[j * PLACES:(j + 1) * PLACES] for one in picked], axis=0)
            rows[j, start:start + 2 * PLACES, :] = both.astype(jnp.bfloat16)
        if s % HALF < 2:
            fetch(s + 2).start()

    def give(k):
        target = expert_peer(position, PEERS[k])
        return pltpu.make_async_remote_copy(
            src_ref=hsend.at[target],
            dst_ref=hidden_ref.at[position],
            send_sem=hsend_sem.at[target],
            recv_sem=hrecv_sem.at[position],
            device_id=(target, place),
            device_id_type=MESH,
        )

    def get(k):
        source = expert_peer(position, PEERS[k])
        return pltpu.make_async_remote_copy(
            src_ref=hsend.at[source],
            dst_ref=hidden_ref.at[source],
            send_sem=hsend_sem.at[source],
            recv_sem=hrecv_sem.at[source],
            device_id=(source, place),
            device_id_type=MESH,
        )

    def project(half):
        for j in range(EXP):
            projected = jnp.dot(rows[j], weights[j // 2], preferred_element_type=jnp.float32)
            start = 180 * (j % 2)
            gate = projected[:, start:start + UNITS]
            up = projected[:, start + UNITS:start + 2 * UNITS]
            hidden = gate / (1.0 + jnp.exp(-gate)) * up
            hidden = jnp.concatenate(
                [hidden, jnp.zeros((HALF * 2 * PLACES, 128 - UNITS), jnp.float32)], axis=1
            )
            turned = jnp.transpose(hidden)[0:96].astype(jnp.bfloat16)
            for s in range(HALF):
                for t in range(2):
                    at = t * EXP * PLACES + j * PLACES
                    part = (2 * s + t) * PLACES
                    hsend[HALF * half + s, :, at:at + PLACES] = turned[:, part:part + PLACES]
        for k in range(7):
            @pl.when(expert_peer(position, PEERS[k]) // HALF == half)
            def _(k=k):
                give(k).start()

    steps = {
        "P": prepare,
        "A": assemble,
        "L": lambda _: gather.line_done(),
        "S": gather.start,
        "N": gather.near,
        "F": gather.far,
        "l": lambda wave: gather.near_lines(wave, (0, 3, 1, 2)),
        "f": gather.far_lines,
        "R": find_rows,
        "C": arrived,
        "G": pick,
        "M": project,
    }
    for step in SCHEDULE:
        steps[step[0]](int(step[1]))
    own_hidden = pltpu.make_async_copy(hsend.at[position], hidden_ref.at[position], hown_sem)
    own_hidden.start()
    for k in range(7):
        for copy in xcopies(k):
            copy.wait()
        routes_copy(k).wait_send()
    for copy in own_copies:
        copy.wait()
    for p in range(PAIRS):
        for offset in FSDP_PEERS:
            piece_copy(p, offset).wait_send()
    gather.end()
    own_hidden.wait()
    for k in range(7):
        get(k).wait_recv()
        give(k).wait_send()


def merge_kernel(from_ref, main_ref, tail_ref, merged_ref, select):
    part = pl.program_id(0)

    @pl.when(part == 0)
    def _():
        to = lax.broadcasted_iota(jnp.int32, (256, 256), 0)
        at = lax.broadcasted_iota(jnp.int32, (256, 256), 1)
        named = jnp.zeros((256, 256), jnp.int32)
        for q in range(SLOTS_DEV):
            named = jnp.where((to & 15) == q, from_ref[q], named)
        inner = 4 * ((at & 31) >> 3) + (at & 3)
        hit = ((to >> 4) == inner) & (named == 2 * (at >> 5) + ((at >> 2) & 1))
        select[...] = hit.astype(jnp.float32).astype(jnp.bfloat16)

    zero = jnp.zeros((), jnp.bfloat16)
    for c in range(4):
        there = lax.broadcasted_iota(jnp.int32, (OWNERS, 32, MAIN), 1) + (part * 128 + c * 32) < 360
        some = jnp.where(there, main_ref[:, 32 * c:32 * c + 32, :], zero)
        put = jnp.dot(select[...], some.reshape(256, MAIN), preferred_element_type=jnp.float32)
        put = put.astype(jnp.bfloat16).reshape(16, SLOTS_DEV, MAIN)
        merged_ref[16 * c:16 * c + 16, :, 0:MAIN] = put
        some = tail_ref[:, 32 * c:32 * c + 32, :].reshape(256, 128)
        put = jnp.dot(select[...], some, preferred_element_type=jnp.float32)
        for g in range(3):
            @pl.when(part == g)
            def _(c=c, g=g, put=put):
                last = put[:, g * TAIL:(g + 1) * TAIL].astype(jnp.bfloat16)
                merged_ref[16 * c:16 * c + 16, :, MAIN:WIDTH] = last.reshape(16, SLOTS_DEV, TAIL)


def combine_kernel(routes_ref, route_weight_ref, base_ref, hidden_ref, out_ref, spread):
    before = (
        lax.broadcasted_iota(jnp.int32, (512, 512), 0) < lax.broadcasted_iota(jnp.int32, (512, 512), 1)
    ).astype(jnp.float32).astype(jnp.bfloat16)
    expert = lax.broadcasted_iota(jnp.int32, (64, 512), 0)
    table = 64 * PLACES
    index = lax.broadcasted_iota(jnp.int32, (table, 512), 0)
    for t in range(2):
        half = slice(t * EXP * PLACES, (t + 1) * EXP * PLACES)
        turned = jnp.concatenate([hidden_ref[s, :, half] for s in range(OWNERS)], axis=1)
        named = [(routes_ref[t, k:k + 1, :] == expert).astype(jnp.float32) for k in range(4)]
        mask = named[0] + named[1] + named[2] + named[3]
        earlier = jnp.dot(mask.astype(jnp.bfloat16), before, preferred_element_type=jnp.float32)
        at = earlier + base_ref[:, 0:1]
        for k in range(4):
            code = jnp.sum(named[k] * at, axis=0, keepdims=True).astype(jnp.int32)
            choose = (index == code).astype(jnp.float32).astype(jnp.bfloat16)
            hidden = jnp.dot(turned, choose, preferred_element_type=jnp.float32)
            weighted = route_weight_ref[t, k:k + 1, :] * hidden[0:UNITS]
            for part in range(4):
                spread[part, pl.ds(k, UNITS, stride=4), :] = weighted[:, part * 128:(part + 1) * 128]
        for part in range(4):
            out_ref[t, :, part * 128:(part + 1) * 128] = spread[part].astype(jnp.bfloat16)


def on_device(tokens, gate_weight, up_weight, slot_of, routes, route_weight):
    position = lax.axis_index("expert")
    ids = jnp.arange(64, dtype=jnp.int32)
    source = ids // EXP
    owner = slot_of // SLOTS_DEV
    step = step_of(source, owner)
    key = step * EXP + ids % EXP
    ahead = (source[None, :] == source[:, None]) & (key[None, :] < key[:, None])
    rank = jnp.sum(ahead.astype(jnp.int32), axis=1)
    within = jnp.sum((ahead & (step[None, :] == step[:, None])).astype(jnp.int32), axis=1)
    at = step * 2 + within
    mine = slot_of[None, :] == (position * SLOTS_DEV + jnp.arange(SLOTS_DEV, dtype=jnp.int32))[:, None]
    from_ = jnp.max(jnp.where(mine, at[None, :], -1), axis=1)
    base = ((source * EXP + rank) * PLACES).astype(jnp.float32)
    base = jnp.broadcast_to(base[:, None], (64, 128))

    routes = jnp.swapaxes(routes, 1, 2)
    route_weight = jnp.swapaxes(route_weight, 1, 2)

    vmem = pl.BlockSpec(memory_space=pltpu.VMEM)
    smem = pl.BlockSpec(memory_space=pltpu.SMEM)
    anyspace = pl.BlockSpec(memory_space=pl.ANY)
    bf16 = jnp.bfloat16
    dma = pltpu.SemaphoreType.DMA
    main, tail, hidden, _ = pl.pallas_call(
        serve_kernel,
        out_shape=(
            jax.ShapeDtypeStruct((OWNERS, 360, MAIN), bf16),
            jax.ShapeDtypeStruct((OWNERS, 128, 128), bf16),
            jax.ShapeDtypeStruct((OWNERS, 96, 2 * EXP * PLACES), bf16),
            jax.ShapeDtypeStruct((2, GROUPS, 4, 2, 32, WIDTH), bf16),
        ),
        in_specs=[smem, anyspace, anyspace, anyspace, anyspace],
        out_specs=(anyspace, anyspace, anyspace, anyspace),
        scratch_shapes=[
            pltpu.VMEM((4, 16, EXP, WIDTH), jnp.float32),
            pltpu.VMEM((2, EXP, 96, WIDTH), bf16),
            pltpu.VMEM((PAIRS, GROUPS, 96, LANES), bf16),
            pltpu.VMEM((PAIRS, GROUPS, 96, LANES), bf16),
            pltpu.VMEM((WIDTH, LANES), jnp.float32),
            pltpu.VMEM((PAIRS, WIDTH, LANES), bf16),
            pltpu.VMEM((PAIRS, 360, MAIN), bf16),
            pltpu.VMEM((PAIRS, 128, 128), bf16),
            pltpu.VMEM((OWNERS, 360, MAIN), bf16),
            pltpu.VMEM((OWNERS, 128, 128), bf16),
            pltpu.VMEM((OWNERS, 2, 4, 512), jnp.int32),
            pltpu.VMEM((16, EXP, 512), jnp.float32),
            pltpu.VMEM((2, GROUPS, 2, 32, WIDTH), bf16),
            pltpu.VMEM((EXP, HALF * 2 * PLACES, WIDTH), bf16),
            pltpu.VMEM((OWNERS, 96, 2 * EXP * PLACES), bf16),
            dma((4,)),
            dma((PAIRS, GROUPS)),
            dma((PAIRS, GROUPS)),
            dma((2, 7)),
            dma((2, 7)),
            dma((2,)),
            dma((7,)),
            dma((OWNERS,)),
            dma,
            dma((2,)),
            dma((OWNERS,)),
            dma((OWNERS,)),
            dma,
            dma((3,)),
            dma((4,)),
            dma,
            dma((80,)),
            dma((WAVES, 2, GROUPS, 2)),
            dma((WAVES, 2, GROUPS)),
            dma((WAVES, 2, GROUPS)),
        ],
        compiler_params=pltpu.CompilerParams(
            collective_id=1, has_side_effects=True, vmem_limit_bytes=VMEM_LIMIT
        ),
        cost_estimate=pl.CostEstimate(flops=12 * 10**9, bytes_accessed=400 * 10**6, transcendentals=10**6),
        name="serve",
    )(slot_of, jnp.swapaxes(gate_weight, 0, 1), jnp.swapaxes(up_weight, 0, 1), routes, tokens)

    merged = pl.pallas_call(
        merge_kernel,
        out_shape=jax.ShapeDtypeStruct((180, SLOTS_DEV, WIDTH), bf16),
        grid_spec=pltpu.PrefetchScalarGridSpec(
            num_scalar_prefetch=1,
            grid=(3,),
            in_specs=[
                pl.BlockSpec((OWNERS, 128, MAIN), lambda i, from_ref: (0, i, 0)),
                pl.BlockSpec((OWNERS, 128, 128), lambda i, from_ref: (0, 0, 0)),
            ],
            out_specs=pl.BlockSpec((64, SLOTS_DEV, WIDTH), lambda i, from_ref: (i, 0, 0)),
            scratch_shapes=[pltpu.VMEM((256, 256), bf16)],
        ),
        compiler_params=pltpu.CompilerParams(vmem_limit_bytes=VMEM_LIMIT),
        name="merge",
    )(from_, main, tail)
    weighted = pl.pallas_call(
        combine_kernel,
        out_shape=jax.ShapeDtypeStruct((2, 4 * UNITS, 512), bf16),
        in_specs=[vmem, vmem, vmem, vmem],
        out_specs=vmem,
        scratch_shapes=[pltpu.VMEM((4, 4 * UNITS, 128), jnp.float32)],
        compiler_params=pltpu.CompilerParams(vmem_limit_bytes=VMEM_LIMIT),
        name="combine",
    )(routes, route_weight, base, hidden)
    weighted = weighted.reshape(2, UNITS, 4, 512)
    return jnp.swapaxes(merged, 0, 1), jnp.transpose(weighted, (0, 3, 2, 1))


def solution(mesh):
    in_specs = (
        P(None, ("expert", "fsdp"), None),
        P("expert", "fsdp", None),
        P("expert", "fsdp", None),
        P(),
        P(None, "expert", None),
        P(None, "expert", None),
    )
    out_specs = (P("expert", "fsdp", None), P(None, "expert", None, "fsdp"))
    return jax.shard_map(
        on_device, mesh=mesh, in_specs=in_specs, out_specs=out_specs, check_vma=False
    )
```

```python
import functools
import jax
import jax.numpy as jnp
from jax import lax
from jax.experimental import pallas as pl
from jax.experimental.pallas import tpu as pltpu
from jax.sharding import PartitionSpec as P

MESH = pl.DeviceIdType.MESH
EXP = 8
PAIRS = 4
GROUPS = 16
OWNERS = 8
SLOTS_DEV = 16
DEPTH = 90
UNITS = 90
WIDTH = 1440
MOST = 36
PLACES = 40
LANES = 384
MAIN = 1408
TAIL = WIDTH - MAIN
HALF = 4
VMEM_LIMIT = 60 << 20
PEERS = ((2, 0), (1, 0), (3, 0), (2, 1), (1, 1), (3, 1), (0, 1), (0, 0))
FSDP_PEERS = (
    (0, 1), (3, 0), (0, 3), (1, 0), (1, 1), (3, 3), (1, 3), (3, 1),
    (2, 0), (0, 2), (2, 1), (1, 2), (2, 3), (3, 2), (2, 2),
)
WAVES = 2
SCHEDULE = (
    "P0", "P1", "P2", "P3", "L0", "S0", "S1", "R0", "A0", "A1", "A2", "A3",
    "N0", "F0", "l0", "N1", "F1", "f0", "l1", "C0", "G0", "G1", "G2", "G3", "f1", "M0",
    "C1", "G4", "G5", "G6", "G7", "M1",
)


def step_of(source, owner):
    dx = ((owner >> 1) - (source >> 1)) & 3
    dc = (owner - source) & 1
    near = jnp.where(dx == 2, 0, jnp.where(dx == 1, 1, 2))
    return jnp.where(dx == 0, 7 - dc, 3 * dc + near)


def expert_peer(position, offset):
    dx, dc = offset
    return ((position // 2 + dx) & 3) * 2 + ((position + dc) & 1)


def fsdp_peer(place, offset):
    dz, dy = offset
    return ((place // 4 + dz) & 3) * 4 + ((place + dy) & 3)


def greet(position, place, with_fsdp):
    barrier = pltpu.get_barrier_semaphore()
    count = 0
    for offset in PEERS[:-1]:
        pl.semaphore_signal(
            barrier, inc=1, device_id=(expert_peer(position, offset), place), device_id_type=MESH
        )
        count += 1
    if with_fsdp:
        for offset in FSDP_PEERS:
            pl.semaphore_signal(
                barrier, inc=1, device_id=(position, fsdp_peer(place, offset)), device_id_type=MESH
            )
            count += 1
    pl.semaphore_wait(barrier, count)


class TokenGather:
    def __init__(self, tokens, everything, line_send, line_recv, own_sem, send, recv, pair_send, pair_recv):
        self.position = lax.axis_index("expert")
        self.place = lax.axis_index("fsdp")
        self.core = self.position & 1
        self.x = self.position // 2
        self.tokens, self.everything = tokens, everything
        self.line_send, self.line_recv, self.own_sem = line_send, line_recv, own_sem
        self.send, self.recv, self.pair_send, self.pair_recv = send, recv, pair_send, pair_recv
        self.count = 0
        self.sent = []

    def line_copy(self, dx, source_dx):
        x = (self.x + source_dx) & 3
        return pltpu.make_async_remote_copy(
            src_ref=self.tokens,
            dst_ref=self.everything.at[self.core, self.place, x],
            send_sem=self.line_send.at[dx - 1],
            recv_sem=self.line_recv.at[x],
            device_id=(((self.x + dx) & 3) * 2 + self.core, self.place),
            device_id_type=MESH,
        )

    def own_copy(self):
        return pltpu.make_async_copy(
            self.tokens, self.everything.at[self.core, self.place, self.x], self.own_sem
        )

    def begin(self):
        for dx in (2, 1, 3):
            self.line_copy(dx, 0).start()
        self.own_copy().start()

    def line_done(self):
        self.own_copy().wait()
        for dx in (1, 2, 3):
            self.line_copy(dx, dx).wait_recv()

    def at(self, kind, first, second):
        return fsdp_peer(self.place, (second, first) if kind == 0 else (first, second))

    def unit(self, wave, kind, f, half, core):
        ref = self.everything.at[core, f, 2 * wave + kind]
        return ref if half is None else ref.at[half]

    def copy(self, wave, kind, f, half, target, index):
        ref = self.unit(wave, kind, f, half, self.core)
        return pltpu.make_async_remote_copy(
            src_ref=ref,
            dst_ref=ref,
            send_sem=self.send.at[index],
            recv_sem=self.recv.at[wave, kind, f, 0 if half is None else half],
            device_id=(self.position, target),
            device_id_type=MESH,
        )

    def give(self, wave, kind, f, half, target):
        copy = self.copy(wave, kind, f, half, target, self.count)
        copy.start()
        self.sent.append(copy)
        self.count += 1

    def arrival(self, wave, kind, f, half):
        self.copy(wave, kind, f, half, self.place, 0).wait_recv()

    def pair_copy(self, wave, kind, f, core):
        ref = self.unit(wave, kind, f, None, core)
        return pltpu.make_async_remote_copy(
            src_ref=ref,
            dst_ref=ref,
            send_sem=self.pair_send.at[wave, kind, f],
            recv_sem=self.pair_recv.at[wave, kind, f],
            device_id=(self.position ^ 1, self.place),
            device_id_type=MESH,
        )

    def share(self, wave, kind, f):
        self.pair_copy(wave, kind, f, self.core).start()

    def across(self, wave, kind, first):
        f = self.at(kind, first, 0)
        for second in (1, 3):
            self.give(wave, kind, f, None, self.at(kind, 0, second))
        self.share(wave, kind, f)

    def start(self, wave):
        for kind in range(2):
            for first in (1, 3):
                self.give(wave, kind, self.place, None, self.at(kind, first, 0))
        for kind in range(2):
            self.across(wave, kind, 0)

    def near(self, wave):
        for kind in range(2):
            for first, half in ((3, 0), (1, 1)):
                f = self.at(kind, first, 0)
                self.arrival(wave, kind, f, None)
                self.give(wave, kind, f, half, self.at(kind, (first + 2) & 3, 0))
        for kind in range(2):
            for first in (3, 1):
                self.across(wave, kind, first)

    def far(self, wave):
        for kind in range(2):
            f = self.at(kind, 2, 0)
            self.arrival(wave, kind, f, 0)
            self.arrival(wave, kind, f, 1)
            self.across(wave, kind, 2)

    def near_lines(self, wave, firsts):
        for first in firsts:
            for kind in range(2):
                for second, half in ((3, 0), (1, 1)):
                    f = self.at(kind, first, second)
                    self.arrival(wave, kind, f, None)
                    self.give(wave, kind, f, half, self.at(kind, 0, (second + 2) & 3))
                    self.share(wave, kind, f)

    def far_lines(self, wave):
        for first in (0, 3, 1, 2):
            for kind in range(2):
                f = self.at(kind, first, 2)
                self.arrival(wave, kind, f, 0)
                self.arrival(wave, kind, f, 1)
                self.share(wave, kind, f)

    def other_core(self, wave):
        for kind in range(2):
            for f in range(GROUPS):
                self.pair_copy(wave, kind, f, 1 - self.core).wait_recv()

    def end(self):
        for dx in (1, 2, 3):
            self.line_copy(dx, 0).wait_send()
        for copy in self.sent:
            copy.wait_send()
        for wave in range(WAVES):
            for kind in range(2):
                for f in range(GROUPS):
                    self.pair_copy(wave, kind, f, self.core).wait_send()


def serve_kernel(
    slot_ref, slots_ref, gate_ref, up_ref, routes_ref, tokens_ref,
    main_ref, tail_ref, hidden_ref, all_tokens_ref, from_ref, base_ref,
    raw, ranked, send, recv, tall, weights, blocks, ends, xsend, xends, all_routes, spots, chunk, rows, hsend,
    load_sem, send_sem, recv_sem, xsend_sem, xrecv_sem, own_sem, rsend_sem, rrecv_sem, rown_sem,
    chunk_sem, hsend_sem, hrecv_sem, hown_sem, *gather_sems,
):
    position = lax.axis_index("expert")
    place = lax.axis_index("fsdp")

    def load(i):
        ref = (gate_ref, up_ref)[i // 6]
        start = 16 * (i % 6)
        depth = min(16, DEPTH - start)
        return pltpu.make_async_copy(
            ref.at[pl.ds(start, depth)], raw.at[i % 4, pl.ds(0, depth)], load_sem.at[i % 4]
        )

    for i in range(4):
        load(i).start()
    greet(position, place, True)
    gather = TokenGather(tokens_ref, all_tokens_ref, *gather_sems)
    gather.begin()

    def routes_copy(k):
        return pltpu.make_async_remote_copy(
            src_ref=routes_ref,
            dst_ref=all_routes.at[position],
            send_sem=rsend_sem.at[k],
            recv_sem=rrecv_sem.at[position],
            device_id=(expert_peer(position, PEERS[k]), place),
            device_id_type=MESH,
        )

    def routes_arrival(k):
        source = expert_peer(position, PEERS[k])
        return pltpu.make_async_remote_copy(
            src_ref=routes_ref,
            dst_ref=all_routes.at[source],
            send_sem=rsend_sem.at[k],
            recv_sem=rrecv_sem.at[source],
            device_id=(source, place),
            device_id_type=MESH,
        )

    for k in range(7):
        routes_copy(k).start()
    own_routes = pltpu.make_async_copy(routes_ref, all_routes.at[position], rown_sem)
    own_routes.start()

    keys = []
    for j in range(EXP):
        owner = slot_ref[position * EXP + j] // SLOTS_DEV
        keys.append(step_of(position, owner) * EXP + j)
    order = [0] * EXP
    step_at = [0] * EXP
    for j in range(EXP):
        rank = 0
        for other in range(EXP):
            if other != j:
                rank = rank + (keys[other] < keys[j]).astype(jnp.int32)
        for i in range(EXP):
            here = (rank == i).astype(jnp.int32)
            order[i] = order[i] + here * j
            step_at[i] = step_at[i] + here * (keys[j] // EXP)
    pair_of = []
    for k in range(OWNERS):
        found = 0
        for p in range(PAIRS):
            found = jnp.where(step_at[2 * p] == k, p, found)
        pair_of.append(found)

    def piece_copy(p, offset):
        target = fsdp_peer(place, offset)
        return pltpu.make_async_remote_copy(
            src_ref=send.at[p, target],
            dst_ref=recv.at[p, place],
            send_sem=send_sem.at[p, target],
            recv_sem=recv_sem.at[p, place],
            device_id=(position, target),
            device_id_type=MESH,
        )

    def piece_arrival(p, offset):
        source = fsdp_peer(place, offset)
        return pltpu.make_async_remote_copy(
            src_ref=send.at[p, source],
            dst_ref=recv.at[p, source],
            send_sem=send_sem.at[p, source],
            recv_sem=recv_sem.at[p, source],
            device_id=(position, source),
            device_id_type=MESH,
        )

    to = lax.broadcasted_iota(jnp.int32, (128, 128), 0)
    at = lax.broadcasted_iota(jnp.int32, (128, 128), 1)
    named = jnp.zeros((128, 128), jnp.int32)
    for i in range(EXP):
        named = jnp.where((to >> 4) == i, order[i], named)
    rank_rows = ((to & 15) == (at >> 3)) & (named == (at & 7))
    rank_rows = rank_rows.astype(jnp.float32).astype(jnp.bfloat16)
    for i in range(12):
        load(i).wait()
        c = i % 6
        depth = min(16, DEPTH - 16 * c)
        some = raw[i % 4, 0:depth].reshape(depth * EXP, WIDTH).astype(jnp.bfloat16)
        put = jnp.dot(rank_rows[:, :depth * EXP], some, preferred_element_type=jnp.float32)
        ranked[i // 6, :, 16 * c:16 * c + 16, :] = put.astype(jnp.bfloat16).reshape(EXP, 16, WIDTH)
        if i + 4 < 12:
            load(i + 4).start()

    pad = jnp.zeros((96, LANES - 4 * UNITS), jnp.bfloat16)

    def prepare(p):
        for f in range(GROUPS):
            units = slice(f * UNITS, (f + 1) * UNITS)
            send[p, f] = jnp.concatenate(
                [
                    ranked[0, 2 * p, :, units],
                    ranked[1, 2 * p, :, units],
                    ranked[0, 2 * p + 1, :, units],
                    ranked[1, 2 * p + 1, :, units],
                    pad,
                ],
                axis=1,
            )
        for offset in FSDP_PEERS:
            piece_copy(p, offset).start()
        recv[p, place] = send[p, place]

    row = lax.broadcasted_iota(jnp.int32, (360, LANES), 0)
    lane = lax.broadcasted_iota(jnp.int32, (360, LANES), 1)
    inner = 4 * (row >> 3) + (row & 3)
    mix = lane == 180 * ((row >> 2) & 1) + 90 * (inner & 1) + (inner >> 1)
    mix = mix.astype(jnp.float32).astype(jnp.bfloat16)

    def xcopies(k):
        peer = (expert_peer(position, PEERS[k]), place)
        return [
            pltpu.make_async_remote_copy(
                src_ref=source.at[k],
                dst_ref=target.at[k],
                send_sem=xsend_sem.at[part, k],
                recv_sem=xrecv_sem.at[part, k],
                device_id=peer,
                device_id_type=MESH,
            )
            for part, (source, target) in enumerate(((xsend, main_ref), (xends, tail_ref)))
        ]

    own_copies = [
        pltpu.make_async_copy(xsend.at[7], main_ref.at[7], own_sem.at[0]),
        pltpu.make_async_copy(xends.at[7], tail_ref.at[7], own_sem.at[1]),
    ]

    def assemble(p):
        for offset in FSDP_PEERS:
            piece_arrival(p, offset).wait_recv()
        for f in range(GROUPS):
            tall[f * DEPTH:(f + 1) * DEPTH, :] = recv[p, f, 0:DEPTH, :].astype(jnp.float32)
        whole = tall[...].astype(jnp.bfloat16)
        weights[p] = whole
        turned = lax.dot_general(
            mix, whole, (((1,), (1,)), ((), ())), preferred_element_type=jnp.float32
        )
        blocks[p] = turned[:, 0:MAIN].astype(jnp.bfloat16)
        last = turned[:, MAIN:WIDTH]
        last = jnp.concatenate(
            [
                last[0:128],
                last[128:256],
                jnp.concatenate([last[256:360], jnp.zeros((24, TAIL), jnp.float32)], axis=0),
                jnp.zeros((128, TAIL), jnp.float32),
            ],
            axis=1,
        )
        ends[p] = last.astype(jnp.bfloat16)
        for k in (p,) if p < PAIRS - 1 else range(PAIRS - 1, OWNERS):
            xsend[k] = blocks[pair_of[k]]
            xends[k] = ends[pair_of[k]]
            for copy in xcopies(k) if k < 7 else own_copies:
                copy.start()

    def make_tables(_):
        across = jnp.broadcast_to(slots_ref[...], (64, 64))
        down = jnp.transpose(across.astype(jnp.float32)).astype(jnp.int32)
        ids_across = lax.broadcasted_iota(jnp.int32, (64, 64), 1)
        ids_down = lax.broadcasted_iota(jnp.int32, (64, 64), 0)

        def step_and_key(slots, ids):
            step = step_of(ids >> 3, slots >> 4)
            return step, step * EXP + (ids & 7)

        step_across, key_across = step_and_key(across, ids_across)
        step_down, key_down = step_and_key(down, ids_down)
        same = (ids_across >> 3) == (ids_down >> 3)
        behind = same & (key_down < key_across) & (step_down == step_across)
        within = jnp.sum(behind.astype(jnp.float32), axis=0, keepdims=True).astype(jnp.int32)
        at = 2 * step_across[0:1] + within
        slot = (lax.broadcasted_iota(jnp.int32, (256, 64), 0) & 15) + position * SLOTS_DEV
        mine = slots_ref[...] == slot
        found = jnp.max(jnp.where(mine, at, -1).astype(jnp.float32), axis=1, keepdims=True)
        from_ref[...] = jnp.broadcast_to(found, (256, 128)).astype(jnp.int32)
        ahead = (same & (key_across < key_down)).astype(jnp.float32)
        rank = jnp.sum(ahead, axis=1, keepdims=True)
        source = (lax.broadcasted_iota(jnp.int32, (64, 1), 0) >> 3).astype(jnp.float32)
        base_ref[...] = jnp.broadcast_to((source * EXP + rank) * PLACES, (64, 128))

    def find_rows(_):
        make_tables(0)
        own_routes.wait()
        for k in range(7):
            routes_arrival(k).wait_recv()
        nth = lax.broadcasted_iota(jnp.int32, (EXP, 512), 0)
        ids = jnp.zeros((EXP, 512), jnp.int32)
        for i in range(EXP):
            ids = jnp.where(nth == i, position * EXP + order[i], ids)
        masks = []
        for s in range(OWNERS):
            for t in range(2):
                named = all_routes[s, t]
                mask = jnp.zeros((EXP, 512), jnp.float32)
                for k in range(4):
                    mask = mask + (named[k:k + 1, :] == ids).astype(jnp.float32)
                masks.append(mask)
        mask = jnp.concatenate(masks, axis=0)
        before = (
            lax.broadcasted_iota(jnp.int32, (512, 512), 0)
            < lax.broadcasted_iota(jnp.int32, (512, 512), 1)
        ).astype(jnp.float32).astype(jnp.bfloat16)
        earlier = jnp.dot(mask.astype(jnp.bfloat16), before, preferred_element_type=jnp.float32)
        spots[...] = jnp.where(mask > 0.5, earlier, -1.0).reshape(16, EXP, 512)

    def fetch(s):
        return pltpu.make_async_copy(
            all_tokens_ref.at[s % 2, :, s // 2], chunk.at[s % 2], chunk_sem.at[s % 2]
        )

    def arrived(wave):
        gather.other_core(wave)
        fetch(HALF * wave).start()
        fetch(HALF * wave + 1).start()

    def pick(s):
        nth = lax.broadcasted_iota(jnp.int32, (EXP, PLACES, 512), 1).astype(jnp.float32)
        fetch(s).wait()
        picked = []
        for t in range(2):
            spot = spots[2 * s + t]
            choose = (spot[:, None, :] == nth).astype(jnp.float32)
            choose = choose.reshape(EXP * PLACES, 512).astype(jnp.bfloat16)
            step_tokens = chunk[s % 2, :, t].reshape(512, WIDTH)
            picked.append(jnp.dot(choose, step_tokens, preferred_element_type=jnp.float32))
        start = (s % HALF) * 2 * PLACES
        for j in range(EXP):
            both = jnp.concatenate([one[j * PLACES:(j + 1) * PLACES] for one in picked], axis=0)
            rows[j, start:start + 2 * PLACES, :] = both.astype(jnp.bfloat16)
        if s % HALF < 2:
            fetch(s + 2).start()

    def give(k):
        target = expert_peer(position, PEERS[k])
        return pltpu.make_async_remote_copy(
            src_ref=hsend.at[target],
            dst_ref=hidden_ref.at[position],
            send_sem=hsend_sem.at[target],
            recv_sem=hrecv_sem.at[position],
            device_id=(target, place),
            device_id_type=MESH,
        )

    def get(k):
        source = expert_peer(position, PEERS[k])
        return pltpu.make_async_remote_copy(
            src_ref=hsend.at[source],
            dst_ref=hidden_ref.at[source],
            send_sem=hsend_sem.at[source],
            recv_sem=hrecv_sem.at[source],
            device_id=(source, place),
            device_id_type=MESH,
        )

    def project(half):
        for j in range(EXP):
            start = 180 * (j % 2)
            low = start // 128 * 128
            projected = jnp.dot(
                rows[j], weights[j // 2, :, low:low + 256], preferred_element_type=jnp.float32
            )
            start = start - low
            gate = projected[:, start:start + UNITS]
            up = projected[:, start + UNITS:start + 2 * UNITS]
            hidden = gate / (1.0 + jnp.exp(-gate)) * up
            hidden = jnp.concatenate(
                [hidden, jnp.zeros((HALF * 2 * PLACES, 128 - UNITS), jnp.float32)], axis=1
            )
            turned = jnp.transpose(hidden)[0:96].astype(jnp.bfloat16)
            for s in range(HALF):
                for t in range(2):
                    at = t * EXP * PLACES + j * PLACES
                    part = (2 * s + t) * PLACES
                    hsend[HALF * half + s, :, at:at + PLACES] = turned[:, part:part + PLACES]
        for k in range(7):
            @pl.when(expert_peer(position, PEERS[k]) // HALF == half)
            def _(k=k):
                give(k).start()

    steps = {
        "P": prepare,
        "A": assemble,
        "L": lambda _: gather.line_done(),
        "S": gather.start,
        "N": gather.near,
        "F": gather.far,
        "l": lambda wave: gather.near_lines(wave, (0, 3, 1, 2)),
        "f": gather.far_lines,
        "R": find_rows,
        "C": arrived,
        "G": pick,
        "M": project,
    }
    for step in SCHEDULE:
        steps[step[0]](int(step[1]))
    own_hidden = pltpu.make_async_copy(hsend.at[position], hidden_ref.at[position], hown_sem)
    own_hidden.start()
    for k in range(7):
        for copy in xcopies(k):
            copy.wait()
        routes_copy(k).wait_send()
    for copy in own_copies:
        copy.wait()
    for p in range(PAIRS):
        for offset in FSDP_PEERS:
            piece_copy(p, offset).wait_send()
    gather.end()
    own_hidden.wait()
    for k in range(7):
        get(k).wait_recv()
        give(k).wait_send()


def finish_kernel(
    from_ref, main_ref, tail_ref, routes_ref, route_weight_ref, base_ref, hidden_ref,
    merged_ref, out_ref, select, spread,
):
    part = pl.program_id(0)

    @pl.when(part == 0)
    def _():
        to = lax.broadcasted_iota(jnp.int32, (256, 256), 0)
        at = lax.broadcasted_iota(jnp.int32, (256, 256), 1)
        named = jnp.concatenate([from_ref[...], from_ref[...]], axis=1)
        inner = 4 * ((at & 31) >> 3) + (at & 3)
        hit = ((to >> 4) == inner) & (named == 2 * (at >> 5) + ((at >> 2) & 1))
        select[...] = hit.astype(jnp.float32).astype(jnp.bfloat16)

    zero = jnp.zeros((), jnp.bfloat16)
    for c in range(4):
        there = lax.broadcasted_iota(jnp.int32, (OWNERS, 32, MAIN), 1) + (part * 128 + c * 32) < 360
        some = jnp.where(there, main_ref[:, 32 * c:32 * c + 32, :], zero)
        put = jnp.dot(select[...], some.reshape(256, MAIN), preferred_element_type=jnp.float32)
        put = put.astype(jnp.bfloat16).reshape(16, SLOTS_DEV, MAIN)
        merged_ref[16 * c:16 * c + 16, :, 0:MAIN] = put
        some = tail_ref[:, 32 * c:32 * c + 32, :].reshape(256, 128)
        put = jnp.dot(select[...], some, preferred_element_type=jnp.float32)
        for g in range(3):
            @pl.when(part == g)
            def _(c=c, g=g, put=put):
                last = put[:, g * TAIL:(g + 1) * TAIL].astype(jnp.bfloat16)
                merged_ref[16 * c:16 * c + 16, :, MAIN:WIDTH] = last.reshape(16, SLOTS_DEV, TAIL)

    @pl.when(part < 2)
    def _():
        t = part
        before = (
            lax.broadcasted_iota(jnp.int32, (512, 512), 0)
            < lax.broadcasted_iota(jnp.int32, (512, 512), 1)
        ).astype(jnp.float32).astype(jnp.bfloat16)
        expert = lax.broadcasted_iota(jnp.int32, (64, 512), 0)
        table = 64 * PLACES
        index = lax.broadcasted_iota(jnp.int32, (table, 512), 0)
        per_step = EXP * PLACES
        turned = jnp.concatenate(
            [
                jnp.where(t == 0, hidden_ref[s, :, 0:per_step], hidden_ref[s, :, per_step:2 * per_step])
                for s in range(OWNERS)
            ],
            axis=1,
        )
        named = [(routes_ref[t, k:k + 1, :] == expert).astype(jnp.float32) for k in range(4)]
        mask = named[0] + named[1] + named[2] + named[3]
        earlier = jnp.dot(mask.astype(jnp.bfloat16), before, preferred_element_type=jnp.float32)
        at = earlier + base_ref[:, 0:1]
        for k in range(4):
            code = jnp.sum(named[k] * at, axis=0, keepdims=True).astype(jnp.int32)
            choose = (index == code).astype(jnp.float32).astype(jnp.bfloat16)
            hidden = jnp.dot(turned, choose, preferred_element_type=jnp.float32)
            weighted = route_weight_ref[t, k:k + 1, :] * hidden[0:UNITS]
            for c in range(4):
                spread[c, pl.ds(k, UNITS, stride=4), :] = weighted[:, c * 128:(c + 1) * 128]
        for c in range(4):
            out_ref[t, :, :, c * 128:(c + 1) * 128] = (
                spread[c].reshape(UNITS, 4, 128).astype(jnp.bfloat16)
            )


def on_device(tokens, gate_weight, up_weight, slot_of, routes, route_weight):
    routes = jnp.swapaxes(routes, 1, 2)
    route_weight = jnp.swapaxes(route_weight, 1, 2)

    vmem = pl.BlockSpec(memory_space=pltpu.VMEM)
    smem = pl.BlockSpec(memory_space=pltpu.SMEM)
    anyspace = pl.BlockSpec(memory_space=pl.ANY)
    bf16 = jnp.bfloat16
    dma = pltpu.SemaphoreType.DMA
    main, tail, hidden, _, from_, base = pl.pallas_call(
        serve_kernel,
        out_shape=(
            jax.ShapeDtypeStruct((OWNERS, 360, MAIN), bf16),
            jax.ShapeDtypeStruct((OWNERS, 128, 128), bf16),
            jax.ShapeDtypeStruct((OWNERS, 96, 2 * EXP * PLACES), bf16),
            jax.ShapeDtypeStruct((2, GROUPS, 4, 2, 32, WIDTH), bf16),
            jax.ShapeDtypeStruct((256, 128), jnp.int32),
            jax.ShapeDtypeStruct((64, 128), jnp.float32),
        ),
        in_specs=[smem, vmem, anyspace, anyspace, anyspace, anyspace],
        out_specs=(anyspace, anyspace, anyspace, anyspace, vmem, vmem),
        scratch_shapes=[
            pltpu.VMEM((4, 16, EXP, WIDTH), jnp.float32),
            pltpu.VMEM((2, EXP, 96, WIDTH), bf16),
            pltpu.VMEM((PAIRS, GROUPS, 96, LANES), bf16),
            pltpu.VMEM((PAIRS, GROUPS, 96, LANES), bf16),
            pltpu.VMEM((WIDTH, LANES), jnp.float32),
            pltpu.VMEM((PAIRS, WIDTH, LANES), bf16),
            pltpu.VMEM((PAIRS, 360, MAIN), bf16),
            pltpu.VMEM((PAIRS, 128, 128), bf16),
            pltpu.VMEM((OWNERS, 360, MAIN), bf16),
            pltpu.VMEM((OWNERS, 128, 128), bf16),
            pltpu.VMEM((OWNERS, 2, 4, 512), jnp.int32),
            pltpu.VMEM((16, EXP, 512), jnp.float32),
            pltpu.VMEM((2, GROUPS, 2, 32, WIDTH), bf16),
            pltpu.VMEM((EXP, HALF * 2 * PLACES, WIDTH), bf16),
            pltpu.VMEM((OWNERS, 96, 2 * EXP * PLACES), bf16),
            dma((4,)),
            dma((PAIRS, GROUPS)),
            dma((PAIRS, GROUPS)),
            dma((2, 7)),
            dma((2, 7)),
            dma((2,)),
            dma((7,)),
            dma((OWNERS,)),
            dma,
            dma((2,)),
            dma((OWNERS,)),
            dma((OWNERS,)),
            dma,
            dma((3,)),
            dma((4,)),
            dma,
            dma((80,)),
            dma((WAVES, 2, GROUPS, 2)),
            dma((WAVES, 2, GROUPS)),
            dma((WAVES, 2, GROUPS)),
        ],
        compiler_params=pltpu.CompilerParams(
            collective_id=1, has_side_effects=True, vmem_limit_bytes=VMEM_LIMIT
        ),
        cost_estimate=pl.CostEstimate(flops=12 * 10**9, bytes_accessed=400 * 10**6, transcendentals=10**6),
        name="serve",
    )(
        slot_of, slot_of.reshape(1, 64),
        jnp.swapaxes(gate_weight, 0, 1), jnp.swapaxes(up_weight, 0, 1), routes, tokens,
    )

    def whole(*shape):
        return pl.BlockSpec(shape, lambda i: (0,) * len(shape))

    merged, weighted = pl.pallas_call(
        finish_kernel,
        grid=(3,),
        out_shape=(
            jax.ShapeDtypeStruct((180, SLOTS_DEV, WIDTH), bf16),
            jax.ShapeDtypeStruct((2, UNITS, 4, 512), bf16),
        ),
        in_specs=[
            whole(256, 128),
            pl.BlockSpec((OWNERS, 128, MAIN), lambda i: (0, i, 0)),
            whole(OWNERS, 128, 128),
            whole(2, 4, 512),
            whole(2, 4, 512),
            whole(64, 128),
            whole(OWNERS, 96, 2 * EXP * PLACES),
        ],
        out_specs=(
            pl.BlockSpec((64, SLOTS_DEV, WIDTH), lambda i: (i, 0, 0)),
            whole(2, UNITS, 4, 512),
        ),
        scratch_shapes=[
            pltpu.VMEM((256, 256), bf16),
            pltpu.VMEM((4, 4 * UNITS, 128), jnp.float32),
        ],
        compiler_params=pltpu.CompilerParams(vmem_limit_bytes=VMEM_LIMIT),
        name="finish",
    )(from_, main, tail, routes, route_weight, base, hidden)
    return jnp.swapaxes(merged, 0, 1), jnp.transpose(weighted, (0, 3, 2, 1))


def solution(mesh):
    in_specs = (
        P(None, ("expert", "fsdp"), None),
        P("expert", "fsdp", None),
        P("expert", "fsdp", None),
        P(),
        P(None, "expert", None),
        P(None, "expert", None),
    )
    out_specs = (P("expert", "fsdp", None), P(None, "expert", None, "fsdp"))
    return jax.shard_map(
        on_device, mesh=mesh, in_specs=in_specs, out_specs=out_specs, check_vma=False
    )
```

```python
import functools
import jax
import jax.numpy as jnp
from jax import lax
from jax.experimental import pallas as pl
from jax.experimental.pallas import tpu as pltpu
from jax.sharding import PartitionSpec as P

MESH = pl.DeviceIdType.MESH
EXP = 8
PAIRS = 4
GROUPS = 16
OWNERS = 8
SLOTS_DEV = 16
DEPTH = 90
UNITS = 90
WIDTH = 1440
MOST = 36
PLACES = 40
LANES = 384
MAIN = 1408
TAIL = WIDTH - MAIN
HALF = 4
VMEM_LIMIT = 60 << 20
PEERS = ((2, 0), (1, 0), (3, 0), (2, 1), (1, 1), (3, 1), (0, 1), (0, 0))
FSDP_PEERS = (
    (0, 1), (3, 0), (0, 3), (1, 0), (1, 1), (3, 3), (1, 3), (3, 1),
    (2, 0), (0, 2), (2, 1), (1, 2), (2, 3), (3, 2), (2, 2),
)
WAVES = 2
SCHEDULE = (
    "P0", "P1", "P2", "P3", "L0", "S0", "S1", "R0", "A0", "A1", "A2", "A3",
    "N0", "F0", "l0", "N1", "F1", "f0", "l1", "O0", "G0", "G1", "C0", "G2", "G3", "f1", "O1", "M0",
    "G4", "G5", "C1", "G6", "G7", "M1",
)


def step_of(source, owner):
    dx = ((owner >> 1) - (source >> 1)) & 3
    dc = (owner - source) & 1
    near = jnp.where(dx == 2, 0, jnp.where(dx == 1, 1, 2))
    return jnp.where(dx == 0, 7 - dc, 3 * dc + near)


def expert_peer(position, offset):
    dx, dc = offset
    return ((position // 2 + dx) & 3) * 2 + ((position + dc) & 1)


def fsdp_peer(place, offset):
    dz, dy = offset
    return ((place // 4 + dz) & 3) * 4 + ((place + dy) & 3)


def greet(position, place, with_fsdp):
    barrier = pltpu.get_barrier_semaphore()
    count = 0
    for offset in PEERS[:-1]:
        pl.semaphore_signal(
            barrier, inc=1, device_id=(expert_peer(position, offset), place), device_id_type=MESH
        )
        count += 1
    if with_fsdp:
        for offset in FSDP_PEERS:
            pl.semaphore_signal(
                barrier, inc=1, device_id=(position, fsdp_peer(place, offset)), device_id_type=MESH
            )
            count += 1
    pl.semaphore_wait(barrier, count)


class TokenGather:
    def __init__(self, tokens, everything, line_send, line_recv, own_sem, send, recv, pair_send, pair_recv):
        self.position = lax.axis_index("expert")
        self.place = lax.axis_index("fsdp")
        self.core = self.position & 1
        self.x = self.position // 2
        self.tokens, self.everything = tokens, everything
        self.line_send, self.line_recv, self.own_sem = line_send, line_recv, own_sem
        self.send, self.recv, self.pair_send, self.pair_recv = send, recv, pair_send, pair_recv
        self.count = 0
        self.sent = []

    def line_copy(self, dx, source_dx):
        x = (self.x + source_dx) & 3
        return pltpu.make_async_remote_copy(
            src_ref=self.tokens,
            dst_ref=self.everything.at[self.core, self.place, x],
            send_sem=self.line_send.at[dx - 1],
            recv_sem=self.line_recv.at[x],
            device_id=(((self.x + dx) & 3) * 2 + self.core, self.place),
            device_id_type=MESH,
        )

    def own_copy(self):
        return pltpu.make_async_copy(
            self.tokens, self.everything.at[self.core, self.place, self.x], self.own_sem
        )

    def begin(self):
        for dx in (2, 1, 3):
            self.line_copy(dx, 0).start()
        self.own_copy().start()

    def line_done(self):
        self.own_copy().wait()
        for dx in (1, 2, 3):
            self.line_copy(dx, dx).wait_recv()

    def at(self, kind, first, second):
        return fsdp_peer(self.place, (second, first) if kind == 0 else (first, second))

    def unit(self, wave, kind, f, half, core):
        ref = self.everything.at[core, f, 2 * wave + kind]
        return ref if half is None else ref.at[half]

    def copy(self, wave, kind, f, half, target, index):
        ref = self.unit(wave, kind, f, half, self.core)
        return pltpu.make_async_remote_copy(
            src_ref=ref,
            dst_ref=ref,
            send_sem=self.send.at[index],
            recv_sem=self.recv.at[wave, kind, f, 0 if half is None else half],
            device_id=(self.position, target),
            device_id_type=MESH,
        )

    def give(self, wave, kind, f, half, target):
        copy = self.copy(wave, kind, f, half, target, self.count)
        copy.start()
        self.sent.append(copy)
        self.count += 1

    def arrival(self, wave, kind, f, half):
        self.copy(wave, kind, f, half, self.place, 0).wait_recv()

    def pair_copy(self, wave, kind, f, core):
        ref = self.unit(wave, kind, f, None, core)
        return pltpu.make_async_remote_copy(
            src_ref=ref,
            dst_ref=ref,
            send_sem=self.pair_send.at[wave, kind, f],
            recv_sem=self.pair_recv.at[wave, kind, f],
            device_id=(self.position ^ 1, self.place),
            device_id_type=MESH,
        )

    def share(self, wave, kind, f):
        self.pair_copy(wave, kind, f, self.core).start()

    def across(self, wave, kind, first):
        f = self.at(kind, first, 0)
        for second in (1, 3):
            self.give(wave, kind, f, None, self.at(kind, 0, second))
        self.share(wave, kind, f)

    def start(self, wave):
        for kind in range(2):
            for first in (1, 3):
                self.give(wave, kind, self.place, None, self.at(kind, first, 0))
        for kind in range(2):
            self.across(wave, kind, 0)

    def near(self, wave):
        for kind in range(2):
            for first, half in ((3, 0), (1, 1)):
                f = self.at(kind, first, 0)
                self.arrival(wave, kind, f, None)
                self.give(wave, kind, f, half, self.at(kind, (first + 2) & 3, 0))
        for kind in range(2):
            for first in (3, 1):
                self.across(wave, kind, first)

    def far(self, wave):
        for kind in range(2):
            f = self.at(kind, 2, 0)
            self.arrival(wave, kind, f, 0)
            self.arrival(wave, kind, f, 1)
            self.across(wave, kind, 2)

    def near_lines(self, wave, firsts):
        for first in firsts:
            for kind in range(2):
                for second, half in ((3, 0), (1, 1)):
                    f = self.at(kind, first, second)
                    self.arrival(wave, kind, f, None)
                    self.give(wave, kind, f, half, self.at(kind, 0, (second + 2) & 3))
                    self.share(wave, kind, f)

    def far_lines(self, wave):
        for first in (0, 3, 1, 2):
            for kind in range(2):
                f = self.at(kind, first, 2)
                self.arrival(wave, kind, f, 0)
                self.arrival(wave, kind, f, 1)
                self.share(wave, kind, f)

    def other_core(self, wave):
        for kind in range(2):
            for f in range(GROUPS):
                self.pair_copy(wave, kind, f, 1 - self.core).wait_recv()

    def end(self):
        for dx in (1, 2, 3):
            self.line_copy(dx, 0).wait_send()
        for copy in self.sent:
            copy.wait_send()
        for wave in range(WAVES):
            for kind in range(2):
                for f in range(GROUPS):
                    self.pair_copy(wave, kind, f, self.core).wait_send()


def serve_kernel(
    slot_ref, slots_ref, gate_ref, up_ref, routes_ref, tokens_ref,
    main_ref, tail_ref, hidden_ref, all_tokens_ref, from_ref, base_ref,
    raw, ranked, send, recv, tall, weights, blocks, ends, xsend, xends, all_routes, spots, chunk, rows, hsend,
    load_sem, send_sem, recv_sem, xsend_sem, xrecv_sem, own_sem, rsend_sem, rrecv_sem, rown_sem,
    chunk_sem, hsend_sem, hrecv_sem, hown_sem, *gather_sems,
):
    position = lax.axis_index("expert")
    place = lax.axis_index("fsdp")

    def load(i):
        ref = (gate_ref, up_ref)[i // 6]
        start = 16 * (i % 6)
        depth = min(16, DEPTH - start)
        return pltpu.make_async_copy(
            ref.at[pl.ds(start, depth)], raw.at[i % 4, pl.ds(0, depth)], load_sem.at[i % 4]
        )

    for i in range(4):
        load(i).start()
    greet(position, place, True)
    gather = TokenGather(tokens_ref, all_tokens_ref, *gather_sems)
    gather.begin()

    def routes_copy(k):
        return pltpu.make_async_remote_copy(
            src_ref=routes_ref,
            dst_ref=all_routes.at[position],
            send_sem=rsend_sem.at[k],
            recv_sem=rrecv_sem.at[position],
            device_id=(expert_peer(position, PEERS[k]), place),
            device_id_type=MESH,
        )

    def routes_arrival(k):
        source = expert_peer(position, PEERS[k])
        return pltpu.make_async_remote_copy(
            src_ref=routes_ref,
            dst_ref=all_routes.at[source],
            send_sem=rsend_sem.at[k],
            recv_sem=rrecv_sem.at[source],
            device_id=(source, place),
            device_id_type=MESH,
        )

    for k in range(7):
        routes_copy(k).start()
    own_routes = pltpu.make_async_copy(routes_ref, all_routes.at[position], rown_sem)
    own_routes.start()

    keys = []
    for j in range(EXP):
        owner = slot_ref[position * EXP + j] // SLOTS_DEV
        keys.append(step_of(position, owner) * EXP + j)
    order = [0] * EXP
    step_at = [0] * EXP
    for j in range(EXP):
        rank = 0
        for other in range(EXP):
            if other != j:
                rank = rank + (keys[other] < keys[j]).astype(jnp.int32)
        for i in range(EXP):
            here = (rank == i).astype(jnp.int32)
            order[i] = order[i] + here * j
            step_at[i] = step_at[i] + here * (keys[j] // EXP)
    pair_of = []
    for k in range(OWNERS):
        found = 0
        for p in range(PAIRS):
            found = jnp.where(step_at[2 * p] == k, p, found)
        pair_of.append(found)

    def piece_copy(p, offset):
        target = fsdp_peer(place, offset)
        return pltpu.make_async_remote_copy(
            src_ref=send.at[p, target],
            dst_ref=recv.at[p, place],
            send_sem=send_sem.at[p, target],
            recv_sem=recv_sem.at[p, place],
            device_id=(position, target),
            device_id_type=MESH,
        )

    def piece_arrival(p, offset):
        source = fsdp_peer(place, offset)
        return pltpu.make_async_remote_copy(
            src_ref=send.at[p, source],
            dst_ref=recv.at[p, source],
            send_sem=send_sem.at[p, source],
            recv_sem=recv_sem.at[p, source],
            device_id=(position, source),
            device_id_type=MESH,
        )

    to = lax.broadcasted_iota(jnp.int32, (128, 128), 0)
    at = lax.broadcasted_iota(jnp.int32, (128, 128), 1)
    named = jnp.zeros((128, 128), jnp.int32)
    for i in range(EXP):
        named = jnp.where((to >> 4) == i, order[i], named)
    rank_rows = ((to & 15) == (at >> 3)) & (named == (at & 7))
    rank_rows = rank_rows.astype(jnp.float32).astype(jnp.bfloat16)
    for i in range(12):
        load(i).wait()
        c = i % 6
        depth = min(16, DEPTH - 16 * c)
        some = raw[i % 4, 0:depth].reshape(depth * EXP, WIDTH).astype(jnp.bfloat16)
        put = jnp.dot(rank_rows[:, :depth * EXP], some, preferred_element_type=jnp.float32)
        ranked[i // 6, :, 16 * c:16 * c + 16, :] = put.astype(jnp.bfloat16).reshape(EXP, 16, WIDTH)
        if i + 4 < 12:
            load(i + 4).start()

    pad = jnp.zeros((96, LANES - 4 * UNITS), jnp.bfloat16)

    def prepare(p):
        for f in range(GROUPS):
            units = slice(f * UNITS, (f + 1) * UNITS)
            send[p, f] = jnp.concatenate(
                [
                    ranked[0, 2 * p, :, units],
                    ranked[1, 2 * p, :, units],
                    ranked[0, 2 * p + 1, :, units],
                    ranked[1, 2 * p + 1, :, units],
                    pad,
                ],
                axis=1,
            )
        for offset in FSDP_PEERS:
            piece_copy(p, offset).start()
        recv[p, place] = send[p, place]

    row = lax.broadcasted_iota(jnp.int32, (360, LANES), 0)
    lane = lax.broadcasted_iota(jnp.int32, (360, LANES), 1)
    inner = 4 * (row >> 3) + (row & 3)
    mix = lane == 180 * ((row >> 2) & 1) + 90 * (inner & 1) + (inner >> 1)
    mix = mix.astype(jnp.float32).astype(jnp.bfloat16)

    def xcopies(k):
        peer = (expert_peer(position, PEERS[k]), place)
        return [
            pltpu.make_async_remote_copy(
                src_ref=source.at[k],
                dst_ref=target.at[k],
                send_sem=xsend_sem.at[part, k],
                recv_sem=xrecv_sem.at[part, k],
                device_id=peer,
                device_id_type=MESH,
            )
            for part, (source, target) in enumerate(((xsend, main_ref), (xends, tail_ref)))
        ]

    own_copies = [
        pltpu.make_async_copy(xsend.at[7], main_ref.at[7], own_sem.at[0]),
        pltpu.make_async_copy(xends.at[7], tail_ref.at[7], own_sem.at[1]),
    ]

    def assemble(p):
        for offset in FSDP_PEERS:
            piece_arrival(p, offset).wait_recv()
        for f in range(GROUPS):
            tall[f * DEPTH:(f + 1) * DEPTH, :] = recv[p, f, 0:DEPTH, :].astype(jnp.float32)
        whole = tall[...].astype(jnp.bfloat16)
        weights[p] = whole
        turned = lax.dot_general(
            mix, whole, (((1,), (1,)), ((), ())), preferred_element_type=jnp.float32
        )
        blocks[p] = turned[:, 0:MAIN].astype(jnp.bfloat16)
        last = turned[:, MAIN:WIDTH]
        last = jnp.concatenate(
            [
                last[0:128],
                last[128:256],
                jnp.concatenate([last[256:360], jnp.zeros((24, TAIL), jnp.float32)], axis=0),
                jnp.zeros((128, TAIL), jnp.float32),
            ],
            axis=1,
        )
        ends[p] = last.astype(jnp.bfloat16)
        for k in (p,) if p < PAIRS - 1 else range(PAIRS - 1, OWNERS):
            xsend[k] = blocks[pair_of[k]]
            xends[k] = ends[pair_of[k]]
            for copy in xcopies(k) if k < 7 else own_copies:
                copy.start()

    def make_tables(_):
        across = jnp.broadcast_to(slots_ref[...], (64, 64))
        down = jnp.transpose(across.astype(jnp.float32)).astype(jnp.int32)
        ids_across = lax.broadcasted_iota(jnp.int32, (64, 64), 1)
        ids_down = lax.broadcasted_iota(jnp.int32, (64, 64), 0)

        def step_and_key(slots, ids):
            step = step_of(ids >> 3, slots >> 4)
            return step, step * EXP + (ids & 7)

        step_across, key_across = step_and_key(across, ids_across)
        step_down, key_down = step_and_key(down, ids_down)
        same = (ids_across >> 3) == (ids_down >> 3)
        behind = same & (key_down < key_across) & (step_down == step_across)
        within = jnp.sum(behind.astype(jnp.float32), axis=0, keepdims=True).astype(jnp.int32)
        at = 2 * step_across[0:1] + within
        slot = (lax.broadcasted_iota(jnp.int32, (256, 64), 0) & 15) + position * SLOTS_DEV
        mine = slots_ref[...] == slot
        found = jnp.max(jnp.where(mine, at, -1).astype(jnp.float32), axis=1, keepdims=True)
        from_ref[...] = jnp.broadcast_to(found, (256, 128)).astype(jnp.int32)
        ahead = (same & (key_across < key_down)).astype(jnp.float32)
        rank = jnp.sum(ahead, axis=1, keepdims=True)
        source = (lax.broadcasted_iota(jnp.int32, (64, 1), 0) >> 3).astype(jnp.float32)
        base_ref[...] = jnp.broadcast_to((source * EXP + rank) * PLACES, (64, 128))

    def find_rows(_):
        make_tables(0)
        own_routes.wait()
        for k in range(7):
            routes_arrival(k).wait_recv()
        nth = lax.broadcasted_iota(jnp.int32, (EXP, 512), 0)
        ids = jnp.zeros((EXP, 512), jnp.int32)
        for i in range(EXP):
            ids = jnp.where(nth == i, position * EXP + order[i], ids)
        masks = []
        for s in range(OWNERS):
            for t in range(2):
                named = all_routes[s, t]
                mask = jnp.zeros((EXP, 512), jnp.float32)
                for k in range(4):
                    mask = mask + (named[k:k + 1, :] == ids).astype(jnp.float32)
                masks.append(mask)
        mask = jnp.concatenate(masks, axis=0)
        before = (
            lax.broadcasted_iota(jnp.int32, (512, 512), 0)
            < lax.broadcasted_iota(jnp.int32, (512, 512), 1)
        ).astype(jnp.float32).astype(jnp.bfloat16)
        earlier = jnp.dot(mask.astype(jnp.bfloat16), before, preferred_element_type=jnp.float32)
        spots[...] = jnp.where(mask > 0.5, earlier, -1.0).reshape(16, EXP, 512)

    def source(half, i):
        core = (position & 1) ^ (i // 2)
        return core, 2 * half + i % 2

    def fetch(half, i):
        core, x = source(half, i)
        return pltpu.make_async_copy(
            all_tokens_ref.at[core, :, x], chunk.at[i % 2], chunk_sem.at[i % 2]
        )

    def own_arrived(half):
        fetch(half, 0).start()
        fetch(half, 1).start()

    def arrived(half):
        gather.other_core(half)
        fetch(half, 2).start()
        fetch(half, 3).start()

    def pick(index):
        half, i = index // HALF, index % HALF
        core, x = source(half, i)
        nth = lax.broadcasted_iota(jnp.int32, (EXP, PLACES, 512), 1).astype(jnp.float32)
        fetch(half, i).wait()
        picked = []
        for t in range(2):
            spot = spots[2 * (2 * x + core) + t]
            choose = (spot[:, None, :] == nth).astype(jnp.float32)
            choose = choose.reshape(EXP * PLACES, 512).astype(jnp.bfloat16)
            step_tokens = chunk[i % 2, :, t].reshape(512, WIDTH)
            picked.append(jnp.dot(choose, step_tokens, preferred_element_type=jnp.float32))
        start = i * 2 * PLACES
        for j in range(EXP):
            both = jnp.concatenate([one[j * PLACES:(j + 1) * PLACES] for one in picked], axis=0)
            rows[j, start:start + 2 * PLACES, :] = both.astype(jnp.bfloat16)

    def give(k):
        target = expert_peer(position, PEERS[k])
        return pltpu.make_async_remote_copy(
            src_ref=hsend.at[target],
            dst_ref=hidden_ref.at[position],
            send_sem=hsend_sem.at[target],
            recv_sem=hrecv_sem.at[position],
            device_id=(target, place),
            device_id_type=MESH,
        )

    def get(k):
        source = expert_peer(position, PEERS[k])
        return pltpu.make_async_remote_copy(
            src_ref=hsend.at[source],
            dst_ref=hidden_ref.at[source],
            send_sem=hsend_sem.at[source],
            recv_sem=hrecv_sem.at[source],
            device_id=(source, place),
            device_id_type=MESH,
        )

    def project(half):
        for j in range(EXP):
            start = 180 * (j % 2)
            low = start // 128 * 128
            projected = jnp.dot(
                rows[j], weights[j // 2, :, low:low + 256], preferred_element_type=jnp.float32
            )
            start = start - low
            gate = projected[:, start:start + UNITS]
            up = projected[:, start + UNITS:start + 2 * UNITS]
            hidden = gate / (1.0 + jnp.exp(-gate)) * up
            hidden = jnp.concatenate(
                [hidden, jnp.zeros((HALF * 2 * PLACES, 128 - UNITS), jnp.float32)], axis=1
            )
            turned = jnp.transpose(hidden)[0:96].astype(jnp.bfloat16)
            for i in range(HALF):
                core, x = source(half, i)
                for t in range(2):
                    at = t * EXP * PLACES + j * PLACES
                    part = (2 * i + t) * PLACES
                    hsend[2 * x + core, :, at:at + PLACES] = turned[:, part:part + PLACES]
        for k in range(7):
            @pl.when(expert_peer(position, PEERS[k]) // HALF == half)
            def _(k=k):
                give(k).start()

    steps = {
        "P": prepare,
        "A": assemble,
        "L": lambda _: gather.line_done(),
        "S": gather.start,
        "N": gather.near,
        "F": gather.far,
        "l": lambda wave: gather.near_lines(wave, (0, 3, 1, 2)),
        "f": gather.far_lines,
        "R": find_rows,
        "O": own_arrived,
        "C": arrived,
        "G": pick,
        "M": project,
    }
    for step in SCHEDULE:
        steps[step[0]](int(step[1]))
    own_hidden = pltpu.make_async_copy(hsend.at[position], hidden_ref.at[position], hown_sem)
    own_hidden.start()
    for k in range(7):
        for copy in xcopies(k):
            copy.wait()
        routes_copy(k).wait_send()
    for copy in own_copies:
        copy.wait()
    for p in range(PAIRS):
        for offset in FSDP_PEERS:
            piece_copy(p, offset).wait_send()
    gather.end()
    own_hidden.wait()
    for k in range(7):
        get(k).wait_recv()
        give(k).wait_send()


def finish_kernel(
    from_ref, main_ref, tail_ref, routes_ref, route_weight_ref, base_ref, hidden_ref,
    merged_ref, out_ref, select, spread,
):
    part = pl.program_id(0)

    @pl.when(part == 0)
    def _():
        to = lax.broadcasted_iota(jnp.int32, (256, 256), 0)
        at = lax.broadcasted_iota(jnp.int32, (256, 256), 1)
        named = jnp.concatenate([from_ref[...], from_ref[...]], axis=1)
        inner = 4 * ((at & 31) >> 3) + (at & 3)
        hit = ((to >> 4) == inner) & (named == 2 * (at >> 5) + ((at >> 2) & 1))
        select[...] = hit.astype(jnp.float32).astype(jnp.bfloat16)

    for c in range(2):
        some = main_ref[:, 32 * c:32 * c + 32, :]
        if c == 1:
            there = lax.broadcasted_iota(jnp.int32, some.shape, 1) + (part * 64 + c * 32) < 360
            some = jnp.where(there, some, jnp.zeros((), jnp.bfloat16))
        put = jnp.dot(select[...], some.reshape(256, MAIN), preferred_element_type=jnp.float32)
        put = put.astype(jnp.bfloat16).reshape(16, SLOTS_DEV, MAIN)
        merged_ref[16 * c:16 * c + 16, :, 0:MAIN] = put
        start = pl.multiple_of((part & 1) * 64 + c * 32, 32)
        some = tail_ref[:, pl.ds(start, 32), :].reshape(256, 128)
        put = jnp.dot(select[...], some, preferred_element_type=jnp.float32)
        for g in range(3):
            @pl.when((part >> 1) == g)
            def _(c=c, g=g, put=put):
                last = put[:, g * TAIL:(g + 1) * TAIL].astype(jnp.bfloat16)
                merged_ref[16 * c:16 * c + 16, :, MAIN:WIDTH] = last.reshape(16, SLOTS_DEV, TAIL)

    @pl.when(part < 2)
    def _():
        t = part
        before = (
            lax.broadcasted_iota(jnp.int32, (512, 512), 0)
            < lax.broadcasted_iota(jnp.int32, (512, 512), 1)
        ).astype(jnp.float32).astype(jnp.bfloat16)
        expert = lax.broadcasted_iota(jnp.int32, (64, 512), 0)
        table = 64 * PLACES
        index = lax.broadcasted_iota(jnp.int32, (table, 512), 0)
        per_step = EXP * PLACES
        turned = jnp.concatenate(
            [
                jnp.where(t == 0, hidden_ref[s, :, 0:per_step], hidden_ref[s, :, per_step:2 * per_step])
                for s in range(OWNERS)
            ],
            axis=1,
        )
        named = [(routes_ref[t, k:k + 1, :] == expert).astype(jnp.float32) for k in range(4)]
        mask = named[0] + named[1] + named[2] + named[3]
        earlier = jnp.dot(mask.astype(jnp.bfloat16), before, preferred_element_type=jnp.float32)
        at = earlier + base_ref[:, 0:1]
        for k in range(4):
            code = jnp.sum(named[k] * at, axis=0, keepdims=True).astype(jnp.int32)
            choose = (index == code).astype(jnp.float32).astype(jnp.bfloat16)
            hidden = jnp.dot(turned, choose, preferred_element_type=jnp.float32)
            weighted = route_weight_ref[t, k:k + 1, :] * hidden[0:UNITS]
            for c in range(4):
                spread[c, pl.ds(k, UNITS, stride=4), :] = weighted[:, c * 128:(c + 1) * 128]
        for c in range(4):
            out_ref[t, :, :, c * 128:(c + 1) * 128] = (
                spread[c].reshape(UNITS, 4, 128).astype(jnp.bfloat16)
            )


def on_device(tokens, gate_weight, up_weight, slot_of, routes, route_weight):
    routes = jnp.swapaxes(routes, 1, 2)
    route_weight = jnp.swapaxes(route_weight, 1, 2)

    vmem = pl.BlockSpec(memory_space=pltpu.VMEM)
    smem = pl.BlockSpec(memory_space=pltpu.SMEM)
    anyspace = pl.BlockSpec(memory_space=pl.ANY)
    bf16 = jnp.bfloat16
    dma = pltpu.SemaphoreType.DMA
    main, tail, hidden, _, from_, base = pl.pallas_call(
        serve_kernel,
        out_shape=(
            jax.ShapeDtypeStruct((OWNERS, 360, MAIN), bf16),
            jax.ShapeDtypeStruct((OWNERS, 128, 128), bf16),
            jax.ShapeDtypeStruct((OWNERS, 96, 2 * EXP * PLACES), bf16),
            jax.ShapeDtypeStruct((2, GROUPS, 4, 2, 32, WIDTH), bf16),
            jax.ShapeDtypeStruct((256, 128), jnp.int32),
            jax.ShapeDtypeStruct((64, 128), jnp.float32),
        ),
        in_specs=[smem, vmem, anyspace, anyspace, anyspace, anyspace],
        out_specs=(anyspace, anyspace, anyspace, anyspace, vmem, vmem),
        scratch_shapes=[
            pltpu.VMEM((4, 16, EXP, WIDTH), jnp.float32),
            pltpu.VMEM((2, EXP, 96, WIDTH), bf16),
            pltpu.VMEM((PAIRS, GROUPS, 96, LANES), bf16),
            pltpu.VMEM((PAIRS, GROUPS, 96, LANES), bf16),
            pltpu.VMEM((WIDTH, LANES), jnp.float32),
            pltpu.VMEM((PAIRS, WIDTH, LANES), bf16),
            pltpu.VMEM((PAIRS, 360, MAIN), bf16),
            pltpu.VMEM((PAIRS, 128, 128), bf16),
            pltpu.VMEM((OWNERS, 360, MAIN), bf16),
            pltpu.VMEM((OWNERS, 128, 128), bf16),
            pltpu.VMEM((OWNERS, 2, 4, 512), jnp.int32),
            pltpu.VMEM((16, EXP, 512), jnp.float32),
            pltpu.VMEM((2, GROUPS, 2, 32, WIDTH), bf16),
            pltpu.VMEM((EXP, HALF * 2 * PLACES, WIDTH), bf16),
            pltpu.VMEM((OWNERS, 96, 2 * EXP * PLACES), bf16),
            dma((4,)),
            dma((PAIRS, GROUPS)),
            dma((PAIRS, GROUPS)),
            dma((2, 7)),
            dma((2, 7)),
            dma((2,)),
            dma((7,)),
            dma((OWNERS,)),
            dma,
            dma((2,)),
            dma((OWNERS,)),
            dma((OWNERS,)),
            dma,
            dma((3,)),
            dma((4,)),
            dma,
            dma((80,)),
            dma((WAVES, 2, GROUPS, 2)),
            dma((WAVES, 2, GROUPS)),
            dma((WAVES, 2, GROUPS)),
        ],
        compiler_params=pltpu.CompilerParams(
            collective_id=1, has_side_effects=True, vmem_limit_bytes=VMEM_LIMIT
        ),
        cost_estimate=pl.CostEstimate(flops=12 * 10**9, bytes_accessed=400 * 10**6, transcendentals=10**6),
        name="serve",
    )(
        slot_of, slot_of.reshape(1, 64),
        jnp.swapaxes(gate_weight, 0, 1), jnp.swapaxes(up_weight, 0, 1), routes, tokens,
    )

    def whole(*shape):
        return pl.BlockSpec(shape, lambda i: (0,) * len(shape))

    merged, weighted = pl.pallas_call(
        finish_kernel,
        grid=(6,),
        out_shape=(
            jax.ShapeDtypeStruct((180, SLOTS_DEV, WIDTH), bf16),
            jax.ShapeDtypeStruct((2, UNITS, 4, 512), bf16),
        ),
        in_specs=[
            whole(256, 128),
            pl.BlockSpec((OWNERS, 64, MAIN), lambda i: (0, i, 0)),
            whole(OWNERS, 128, 128),
            whole(2, 4, 512),
            whole(2, 4, 512),
            whole(64, 128),
            whole(OWNERS, 96, 2 * EXP * PLACES),
        ],
        out_specs=(
            pl.BlockSpec((32, SLOTS_DEV, WIDTH), lambda i: (i, 0, 0)),
            whole(2, UNITS, 4, 512),
        ),
        scratch_shapes=[
            pltpu.VMEM((256, 256), bf16),
            pltpu.VMEM((4, 4 * UNITS, 128), jnp.float32),
        ],
        compiler_params=pltpu.CompilerParams(vmem_limit_bytes=VMEM_LIMIT),
        name="finish",
    )(from_, main, tail, routes, route_weight, base, hidden)
    return jnp.swapaxes(merged, 0, 1), jnp.transpose(weighted, (0, 3, 2, 1))


def solution(mesh):
    in_specs = (
        P(None, ("expert", "fsdp"), None),
        P("expert", "fsdp", None),
        P("expert", "fsdp", None),
        P(),
        P(None, "expert", None),
        P(None, "expert", None),
    )
    out_specs = (P("expert", "fsdp", None), P(None, "expert", None, "fsdp"))
    return jax.shard_map(
        on_device, mesh=mesh, in_specs=in_specs, out_specs=out_specs, check_vma=False
    )
```
